512 devices in a mesh: brow: 16 (over z), bcol: 32 (over y, x, core).
Axes of the slice: x: 4, y: 4, z: 16, core: 2. Of those that a mesh axis runs over, the one named last changes fastest.
Arguments:
- ancestor_cov: bfloat16 [5632, 5632], P('brow', 'bcol'), may hold values from -1 to 4
- ancestor_pattern: int32 [22], replicated, may hold values 0 or 1
- parent_panel: bfloat16 [5632, 4096], P('brow'), may hold values from -0.5 to 0.5
- parent_inverse: bfloat16 [4096, 4096], P('brow', 'bcol'), may hold values from -1 to 4
- child_pattern: int32 [16], replicated, may hold values 0 or 1
- child_panel: bfloat16 [4096, 4096], P('brow', 'bcol'), may hold values from -0.3125 to 0.3125
- child_inverse: bfloat16 [4096, 4096], P('brow', 'bcol'), may hold values from -1 to 4
Outputs:
- ancestor_block: bfloat16 [5632, 4096], P('brow', 'bcol')
- parent_diag: bfloat16 [4096, 4096], P('brow', 'bcol')
- parent_child: bfloat16 [4096, 4096], P('brow', 'bcol')
- child_diag: bfloat16 [4096, 4096], P('brow', 'bcol')
The draws below stay inside these ranges and needn't reach their ends.
All inputs are finite; a program needn't handle non-finite values.
Results may differ from the reference program's by a relative error of at most 0.006.
Values may be sent and summed in bfloat16 or wider, within the bound.
No kernel may reach another device: no remote copies, remote signals or barrier semaphores. Data moves between devices by JAX's collectives and lax.ppermute only.
A program may use at most 64 MiB of HBM per device.

```python
import math
import jax
import jax.numpy as jnp
from jax import lax

BLOCK = 256
WIDTH = 4096
ANC_BLOCKS = 22
ANC = 5632
SN_BLOCKS = 16


def covariance_like(key, extent, low, high, spread):
    scale_key, noise_key = jax.random.split(key)
    logs = jax.random.uniform(scale_key, (extent,), jnp.float32, math.log(low), math.log(high))
    noise = jax.random.normal(noise_key, (extent, extent), jnp.float32)
    scales = jnp.exp(logs)
    noise = (noise + noise.T) * 0.7071
    roots = jnp.sqrt(scales)
    rows_ids = lax.broadcasted_iota(jnp.int32, (extent, extent), 0)
    cols_ids = lax.broadcasted_iota(jnp.int32, (extent, extent), 1)
    diagonal = (rows_ids == cols_ids).astype(jnp.float32)
    coupling = roots[:, None] * roots[None, :] * (spread / math.sqrt(extent)) * jnp.clip(noise, -5.0, 5.0)
    return coupling * (1.0 - diagonal) + diagonal * scales[:, None]


def draw_ancestor_cov(key, part):
    return covariance_like(jax.random.fold_in(key, 11), ANC, 0.5, 2.0, 0.5).astype(jnp.bfloat16)


def draw_parent_inverse(key, part):
    return covariance_like(jax.random.fold_in(key, 23), WIDTH, 0.5, 2.0, 0.5).astype(jnp.bfloat16)


def draw_child_inverse(key, part):
    return covariance_like(jax.random.fold_in(key, 37), WIDTH, 0.5, 2.0, 0.5).astype(jnp.bfloat16)


def plant(values, key, smallest, high):
    place = [jax.random.randint(jax.random.fold_in(key, axis), (), 0, length) for axis, length in enumerate(values.shape)]
    widest = values.shape.index(max(values.shape))
    beside = place[:widest] + [(place[widest] + 1) % values.shape[widest]] + place[widest + 1:]
    return values.at[tuple(place)].set(smallest).at[tuple(beside)].set(high)


def steps_of(own_key, dims, pieces, smallest, high):
    def one(axis_at, parts):
        draws = jax.random.uniform(jax.random.fold_in(jax.random.fold_in(own_key, 6), axis_at), (parts,), jnp.float32, smallest / len(pieces), high / len(pieces))
        return jnp.repeat(jnp.exp(draws), dims[axis_at] // parts).reshape((-1,) + (1,) * (len(dims) - axis_at - 1))

    factor_of = one(*pieces[0])
    for cut in pieces[1:]:
        factor_of = factor_of * one(*cut)
    return factor_of


def normal_values(own_key, dims, scale, reach, cuts=(), held_as=jnp.bfloat16):
    gain = steps_of(own_key, dims, cuts, -0.22, 0.18) if cuts else 1.0
    array = jax.random.normal(own_key, dims, jnp.float32) * scale * gain
    return jnp.minimum(jnp.maximum(array, -reach), reach).astype(held_as)


def setup_inputs(seed: int = 0) -> dict:
    keys = jax.random.split(jax.random.key(seed), 8)
    return {
        "ancestor_cov": draw_ancestor_cov(jax.random.fold_in(keys[7], 71), 0),
        "ancestor_pattern": plant((jax.random.randint(keys[1], (ANC_BLOCKS,), 0, 3) < 2).astype(jnp.int32), jax.random.fold_in(keys[1], 1), 0, 1),
        "parent_panel": normal_values(keys[2], (ANC, WIDTH), (2.6 / ANC ** 0.5), 0.5, ((0, 16),)),
        "parent_inverse": draw_parent_inverse(jax.random.fold_in(keys[7], 71), 0),
        "child_pattern": plant((jax.random.randint(keys[4], (SN_BLOCKS,), 0, 2) < 1).astype(jnp.int32), jax.random.fold_in(keys[4], 1), 0, 1),
        "child_panel": normal_values(keys[5], (WIDTH, WIDTH), (1.3 / WIDTH ** 0.5), 0.3125, ((0, 16), (1, 32))),
        "child_inverse": draw_child_inverse(jax.random.fold_in(keys[7], 71), 0),
    }


def reference(ancestor_cov, ancestor_pattern, parent_panel, parent_inverse, child_pattern, child_panel, child_inverse):
    ancestor_keep = jnp.repeat(ancestor_pattern, BLOCK)
    child_keep = jnp.repeat(child_pattern, BLOCK)
    parent_masked = parent_panel * ancestor_keep[:, None].astype(parent_panel.dtype)
    child_masked = child_panel * child_keep[:, None].astype(child_panel.dtype)
    product = jnp.dot(ancestor_cov, parent_masked, preferred_element_type=jnp.float32)
    ancestor_block = (-product * ancestor_keep[:, None].astype(jnp.float32)).astype(jnp.bfloat16)
    inner = jnp.dot(parent_masked.T, ancestor_block, preferred_element_type=jnp.float32)
    parent_diag = (parent_inverse.astype(jnp.float32) - inner).astype(jnp.bfloat16)
    product = jnp.dot(parent_diag, child_masked, preferred_element_type=jnp.float32)
    parent_child = (-product * child_keep[:, None].astype(jnp.float32)).astype(jnp.bfloat16)
    inner = jnp.dot(child_masked.T, parent_child, preferred_element_type=jnp.float32)
    child_diag = (child_inverse.astype(jnp.float32) - inner).astype(jnp.bfloat16)
    return ancestor_block, parent_diag, parent_child, child_diag
```

```python
import jax
import jax.numpy as jnp
from jax import lax
from jax.experimental import pallas as pl
from jax.experimental.pallas import tpu as pltpu
from jax.sharding import Mesh, PartitionSpec as P

BF = jnp.bfloat16
F32 = jnp.float32
VMEM = pl.BlockSpec(memory_space=pltpu.VMEM)
SMEM = pl.BlockSpec(memory_space=pltpu.SMEM)
Z = ("zh", "zl")
PLANE = ("y", "x", "c")


def block_keep(pattern, first_row, count, total_rows):
    block_rows = total_rows // pattern.shape[0]
    row_ids = first_row + lax.iota(jnp.int32, count)
    block_ids = lax.iota(jnp.int32, pattern.shape[0])
    matches = row_ids[:, None] // block_rows == block_ids[None, :]
    return jnp.sum(jnp.where(matches, pattern[None, :], 0), axis=1)


def call(kernel, outs, args, flops):
    specs = [SMEM if a.dtype == jnp.int32 else VMEM for a in args]
    size = sum(a.size * a.dtype.itemsize for a in args)
    size += sum(o.size * o.dtype.itemsize for o in outs)
    return pl.pallas_call(
        kernel,
        out_shape=outs,
        in_specs=specs,
        out_specs=[VMEM] * len(outs),
        compiler_params=pltpu.CompilerParams(vmem_limit_bytes=40 * 1024 * 1024),
        cost_estimate=pl.CostEstimate(flops=flops, bytes_accessed=size, transcendentals=0),
    )(*args)


def image_kernel(classes, at_ref, panel_ref, own_ref, right_ref, left_ref, far_ref):
    at = at_ref[...]
    for n, out in enumerate((right_ref, left_ref, far_ref, own_ref)):
        for rh in range(4):
            start = pl.multiple_of((4 * rh + classes[n]) * 256, 256)
            block = jnp.dot(at, panel_ref[:, pl.ds(start, 256)], preferred_element_type=F32)
            out[rh] = block.astype(out.dtype)


def panel_kernel(left_ref, blocks_ref, out_ref):
    rows = left_ref.shape[0] // 4
    total = None
    for h in range(4):
        right = jnp.concatenate([blocks_ref[4 * h + n, :rows, :] for n in range(4)], axis=1)
        part = lax.dot_general(
            left_ref[h * rows : (h + 1) * rows, :],
            right,
            (((0,), (0,)), ((), ())),
            preferred_element_type=F32,
        )
        total = part if total is None else total + part
    for n in range(4):
        out_ref[n] = total[:, n * 128 : (n + 1) * 128].astype(out_ref.dtype)


def child_kernel(left_ref, blocks_ref, out_ref):
    total = None
    for h in range(4):
        right = jnp.concatenate([blocks_ref[4 * h + n, 352:608, :] for n in range(4)], axis=1)
        left = jnp.concatenate([left_ref[2 * h], left_ref[2 * h + 1]], axis=1)
        part = jnp.dot(left, right, preferred_element_type=F32)
        total = part if total is None else total + part
    for n in range(4):
        out_ref[n] = total[:, n * 128 : (n + 1) * 128].astype(out_ref.dtype)


def last_kernel(factor_ref, image_ref, out_ref):
    for y in range(4):
        total = None
        for x in range(4):
            n = (y * 4 + x) * 2
            left = jnp.concatenate([factor_ref[n], factor_ref[n + 1]], axis=1)
            part = lax.dot_general(
                left, image_ref[x], (((0,), (0,)), ((), ())), preferred_element_type=F32
            )
            total = part if total is None else total + part
        out_ref[y] = total.astype(out_ref.dtype)


def shift(value, by):
    return lax.ppermute(value, Z, [(i, (i + by) % 16) for i in range(16)])


def exchange(value, axis):
    return lax.all_to_all(value, axis, split_axis=0, concat_axis=0, tiled=True)


def after(value, *others):
    return lax.optimization_barrier((value, *others))[0]


def per_device(
    ancestor_cov,
    ancestor_pattern,
    parent_panel,
    parent_inverse,
    child_pattern,
    child_panel,
    child_inverse,
):
    z = lax.axis_index(Z)
    zl = lax.axis_index("zl")
    column = lax.axis_index(PLANE)
    ancestor_keep = block_keep(ancestor_pattern, z * 352, 352, 5632)
    child_keep = block_keep(child_pattern, z * 256, 256, 4096)
    slab = lax.dynamic_slice_in_dim(parent_panel, column * 128, 128, 1)
    slab = slab * ancestor_keep[:, None].astype(BF)
    child_masked = child_panel * child_keep[:, None].astype(BF)
    cov = (ancestor_cov * ancestor_keep[:, None].astype(BF)).T

    swapped = lax.ppermute(
        jnp.concatenate([slab, child_masked], axis=0),
        ("zl", "x"),
        [(a * 4 + b, b * 4 + a) for a in range(4) for b in range(4)],
    )
    blocks = lax.all_gather(swapped, Z, axis=0)

    classes = jnp.stack([(zl + 1) % 4, (zl + 3) % 4, (zl + 2) % 4, zl]).astype(jnp.int32)
    bundle = jax.ShapeDtypeStruct((4, 176, 256), BF)
    own, right, left, far = call(
        image_kernel,
        [jax.ShapeDtypeStruct((4, 176, 256), F32), bundle, bundle, bundle],
        [classes, cov, parent_panel],
        2 * 176 * 352 * 4096,
    )
    right, left = shift(right, 1), shift(left, -1)
    far = jnp.concatenate([shift(far[:2], 2), shift(far[2:], -2)], axis=0)
    image = own + right.astype(F32) + left.astype(F32) + far.astype(F32)
    image = exchange(image.astype(BF), "zh")
    image = jnp.sum(image.astype(F32), axis=0).astype(BF)

    cov_wide = lax.all_gather(cov, ("y", "c"), axis=0, tiled=True)
    image_wide = lax.all_gather(image, ("y", "c"), axis=0, tiled=True)
    factor = lax.all_gather(after(swapped[352:], image), PLANE, axis=0)

    (inner,) = call(
        panel_kernel,
        [jax.ShapeDtypeStruct((4, 256, 128), F32)],
        [image_wide, blocks],
        2 * 1408 * 256 * 512,
    )
    inner = jnp.sum(exchange(inner, "x"), axis=0)
    parent_diag = (parent_inverse.astype(F32) + inner).astype(BF)

    diag_wide = lax.all_gather(parent_diag, ("y", "c"), axis=0)
    (product,) = call(
        child_kernel,
        [jax.ShapeDtypeStruct((4, 256, 128), F32)],
        [diag_wide, blocks],
        2 * 1024 * 256 * 512,
    )
    product = jnp.sum(exchange(product, "x"), axis=0)
    parent_child = (-product * child_keep[:, None].astype(F32)).astype(BF)

    child_wide = lax.all_gather(parent_child, "zl", axis=0)

    (product,) = call(
        panel_kernel,
        [jax.ShapeDtypeStruct((4, 352, 128), F32)],
        [cov_wide, blocks],
        2 * 1408 * 352 * 512,
    )
    product = jnp.sum(exchange(after(product, child_wide), "x"), axis=0)
    ancestor_block = (-product * ancestor_keep[:, None].astype(F32)).astype(BF)

    (inner,) = call(
        last_kernel,
        [jax.ShapeDtypeStruct((4, 256, 128), BF)],
        [factor, child_wide],
        2 * 1024 * 1024 * 128,
    )
    inner = jnp.sum(exchange(inner, "zh").astype(F32), axis=0)
    child_diag = (child_inverse.astype(F32) - inner).astype(BF)
    return (ancestor_block, parent_diag, parent_child, child_diag)


def solution(mesh):
    fine = Mesh(mesh.devices.reshape(4, 4, 4, 4, 2), ("zh", "zl", "y", "x", "c"))
    blocked = P(Z, PLANE)
    return jax.shard_map(
        per_device,
        mesh=fine,
        in_specs=(blocked, P(), P(Z, None), blocked, P(), blocked, blocked),
        out_specs=(blocked, blocked, blocked, blocked),
        check_vma=False,
    )
```

```python
import jax
import jax.numpy as jnp
from jax import lax
from jax.experimental import pallas as pl
from jax.experimental.pallas import tpu as pltpu
from jax.sharding import Mesh, PartitionSpec as P

BF = jnp.bfloat16
F32 = jnp.float32
VMEM = pl.BlockSpec(memory_space=pltpu.VMEM)
SMEM = pl.BlockSpec(memory_space=pltpu.SMEM)
Z = ("zh", "zl")
PLANE = ("y", "x", "c")


def block_keep(pattern, first_row, count, total_rows):
    block_rows = total_rows // pattern.shape[0]
    row_ids = first_row + lax.iota(jnp.int32, count)
    block_ids = lax.iota(jnp.int32, pattern.shape[0])
    matches = row_ids[:, None] // block_rows == block_ids[None, :]
    return jnp.sum(jnp.where(matches, pattern[None, :], 0), axis=1)


def call(kernel, outs, args, flops):
    specs = [SMEM if a.dtype == jnp.int32 else VMEM for a in args]
    size = sum(a.size * a.dtype.itemsize for a in args)
    size += sum(o.size * o.dtype.itemsize for o in outs)
    return pl.pallas_call(
        kernel,
        out_shape=outs,
        in_specs=specs,
        out_specs=[VMEM] * len(outs),
        compiler_params=pltpu.CompilerParams(vmem_limit_bytes=40 * 1024 * 1024),
        cost_estimate=pl.CostEstimate(flops=flops, bytes_accessed=size, transcendentals=0),
    )(*args)


def image_kernel(classes, at_ref, panel_ref, own_ref, right_ref, left_ref, far_ref):
    at = at_ref[...]
    for n, out in enumerate((right_ref, left_ref, far_ref, own_ref)):
        for rh in range(4):
            start = pl.multiple_of((4 * rh + classes[n]) * 256, 256)
            block = jnp.dot(at, panel_ref[:, pl.ds(start, 256)], preferred_element_type=F32)
            out[rh] = block.astype(out.dtype)


def panel_kernel(left_ref, blocks_ref, out_ref):
    rows = left_ref.shape[0] // 4
    total = None
    for h in range(4):
        right = jnp.concatenate([blocks_ref[4 * h + n, :rows, :] for n in range(4)], axis=1)
        part = lax.dot_general(
            left_ref[h * rows : (h + 1) * rows, :],
            right,
            (((0,), (0,)), ((), ())),
            preferred_element_type=F32,
        )
        total = part if total is None else total + part
    for n in range(4):
        out_ref[n] = total[:, n * 128 : (n + 1) * 128].astype(out_ref.dtype)


def products_kernel(cov_ref, diag_ref, blocks_ref, out_ref):
    for first, rows in ((0, 352), (352, 256)):
        total = None
        for h in range(4):
            columns = [blocks_ref[4 * h + n, first : first + rows, :] for n in range(4)]
            right = jnp.concatenate(columns, axis=1)
            if first == 0:
                part = lax.dot_general(
                    cov_ref[h * 352 : (h + 1) * 352, :],
                    right,
                    (((0,), (0,)), ((), ())),
                    preferred_element_type=F32,
                )
            else:
                left = jnp.concatenate([diag_ref[2 * h], diag_ref[2 * h + 1]], axis=1)
                part = jnp.dot(left, right, preferred_element_type=F32)
            total = part if total is None else total + part
        for n in range(4):
            tile = total[:, n * 128 : (n + 1) * 128].astype(out_ref.dtype)
            out_ref[n, first : first + rows, :] = tile


def last_kernel(factor_ref, image_ref, out_ref):
    for x in range(4):
        total = None
        for y in range(4):
            left = jnp.concatenate([factor_ref[y, x, 0], factor_ref[y, x, 1]], axis=1)
            part = lax.dot_general(
                left, image_ref[y], (((0,), (0,)), ((), ())), preferred_element_type=F32
            )
            total = part if total is None else total + part
        out_ref[x] = total.astype(out_ref.dtype)


def shift(value, by):
    return lax.ppermute(value, Z, [(i, (i + by) % 16) for i in range(16)])


def swap(value, first, second):
    pairs = [(a * 4 + b, b * 4 + a) for a in range(4) for b in range(4)]
    return lax.ppermute(value, (first, second), pairs)


def exchange(value, axis):
    return lax.all_to_all(value, axis, split_axis=0, concat_axis=0, tiled=True)


def after(value, *others):
    return lax.optimization_barrier((value, *others))[0]


def per_device(
    ancestor_cov,
    ancestor_pattern,
    parent_panel,
    parent_inverse,
    child_pattern,
    child_panel,
    child_inverse,
):
    z = lax.axis_index(Z)
    zl = lax.axis_index("zl")
    column = lax.axis_index(PLANE)

    slab = lax.dynamic_slice_in_dim(parent_panel, column * 128, 128, 1)
    swapped = swap(jnp.concatenate([slab, child_panel], axis=0), "zl", "x")

    ancestor_keep = block_keep(ancestor_pattern, z * 352, 352, 5632)
    column_keep = block_keep(ancestor_pattern, column * 176, 176, 5632)
    child_keep = block_keep(child_pattern, z * 256, 256, 4096)
    child_column_keep = block_keep(child_pattern, column * 128, 128, 4096)
    cov = ancestor_cov * ancestor_keep[:, None].astype(BF) * column_keep[None, :].astype(BF)
    cov = cov.T

    classes = jnp.stack([(zl + 1) % 4, (zl + 3) % 4, (zl + 2) % 4, zl]).astype(jnp.int32)
    bundle = jax.ShapeDtypeStruct((4, 176, 256), BF)
    own, right, left, far = call(
        image_kernel,
        [jax.ShapeDtypeStruct((4, 176, 256), F32), bundle, bundle, bundle],
        [classes, cov, parent_panel],
        2 * 176 * 352 * 4096,
    )
    blocks = lax.all_gather(after(swapped, own), Z, axis=0)
    right, left = shift(right, 1), shift(left, -1)
    far = jnp.concatenate([shift(far[:2], 2), shift(far[2:], -2)], axis=0)
    factor = swap(after(child_panel, own), "zh", "y")
    image = own + right.astype(F32) + left.astype(F32) + far.astype(F32)
    image = image.astype(BF)

    cov_wide = lax.all_gather(after(cov, image), ("y", "c"), axis=0, tiled=True)
    factor = lax.all_gather(after(factor, image), "c", axis=0)
    factor = lax.all_gather(factor, "x", axis=0)
    image = after(exchange(image, "zh"), cov_wide, factor)
    image = jnp.sum(image.astype(F32), axis=0).astype(BF)
    factor = lax.all_gather(after(factor, image), "y", axis=0)
    image_wide = lax.all_gather(image, ("y", "c"), axis=0, tiled=True)

    (inner,) = call(
        panel_kernel,
        [jax.ShapeDtypeStruct((4, 256, 128), BF)],
        [image_wide, blocks],
        2 * 1408 * 256 * 512,
    )
    inner = jnp.sum(exchange(inner, "x").astype(F32), axis=0)
    parent_diag = (parent_inverse.astype(F32) + inner).astype(BF)

    diag_wide = parent_diag * child_column_keep[None, :].astype(BF)
    diag_wide = lax.all_gather(diag_wide, ("y", "c"), axis=0)
    (product,) = call(
        products_kernel,
        [jax.ShapeDtypeStruct((4, 608, 128), BF)],
        [cov_wide, diag_wide, blocks],
        2 * (1408 * 352 + 1024 * 256) * 512,
    )
    product = -jnp.sum(exchange(product, "x").astype(F32), axis=0)
    ancestor_block = (product[:352] * ancestor_keep[:, None].astype(F32)).astype(BF)
    parent_child = (product[352:] * child_keep[:, None].astype(F32)).astype(BF)

    child_wide = lax.all_gather(parent_child, "zh", axis=0)
    (inner,) = call(
        last_kernel,
        [jax.ShapeDtypeStruct((4, 256, 128), BF)],
        [factor, child_wide],
        2 * 1024 * 1024 * 128,
    )
    inner = jnp.sum(exchange(inner, "zl").astype(F32), axis=0)
    child_diag = (child_inverse.astype(F32) - inner).astype(BF)
    return (ancestor_block, parent_diag, parent_child, child_diag)


def solution(mesh):
    fine = Mesh(mesh.devices.reshape(4, 4, 4, 4, 2), ("zh", "zl", "y", "x", "c"))
    blocked = P(Z, PLANE)
    return jax.shard_map(
        per_device,
        mesh=fine,
        in_specs=(blocked, P(), P(Z, None), blocked, P(), blocked, blocked),
        out_specs=(blocked, blocked, blocked, blocked),
        check_vma=False,
    )
```

```python
import jax
import jax.numpy as jnp
from jax import lax
from jax.experimental import pallas as pl
from jax.experimental.pallas import tpu as pltpu
from jax.sharding import Mesh, PartitionSpec as P

BF = jnp.bfloat16
F32 = jnp.float32
VMEM = pl.BlockSpec(memory_space=pltpu.VMEM)
SMEM = pl.BlockSpec(memory_space=pltpu.SMEM)
Z = ("zh", "zl")
PLANE = ("y", "x", "c")


def block_keep(pattern, first_row, count, total_rows):
    block_rows = total_rows // pattern.shape[0]
    row_ids = first_row + lax.iota(jnp.int32, count)
    block_ids = lax.iota(jnp.int32, pattern.shape[0])
    matches = row_ids[:, None] // block_rows == block_ids[None, :]
    return jnp.sum(jnp.where(matches, pattern[None, :], 0), axis=1)


def call(kernel, outs, args, flops):
    specs = [SMEM if a.dtype == jnp.int32 else VMEM for a in args]
    size = sum(a.size * a.dtype.itemsize for a in args)
    size += sum(o.size * o.dtype.itemsize for o in outs)
    return pl.pallas_call(
        kernel,
        out_shape=outs,
        in_specs=specs,
        out_specs=[VMEM] * len(outs),
        compiler_params=pltpu.CompilerParams(vmem_limit_bytes=40 * 1024 * 1024),
        cost_estimate=pl.CostEstimate(flops=flops, bytes_accessed=size, transcendentals=0),
    )(*args)


def image_kernel(classes, at_ref, panel_ref, own_ref, right_ref, left_ref, far_ref):
    at = at_ref[...]
    for n, out in enumerate((right_ref, left_ref, far_ref, own_ref)):
        for rh in range(4):
            start = pl.multiple_of((4 * rh + classes[n]) * 256, 256)
            block = jnp.dot(at, panel_ref[:, pl.ds(start, 256)], preferred_element_type=F32)
            out[rh] = block.astype(out.dtype)


def panel_kernel(left_ref, blocks_ref, out_ref):
    rows = left_ref.shape[0] // 4
    total = None
    for h in range(4):
        right = jnp.concatenate([blocks_ref[4 * h + n, :rows, :] for n in range(4)], axis=1)
        part = lax.dot_general(
            left_ref[h * rows : (h + 1) * rows, :],
            right,
            (((0,), (0,)), ((), ())),
            preferred_element_type=F32,
        )
        total = part if total is None else total + part
    for n in range(4):
        out_ref[n] = total[:, n * 128 : (n + 1) * 128].astype(out_ref.dtype)


def products_kernel(cov_ref, diag_ref, blocks_ref, out_ref):
    for first, rows in ((0, 352), (352, 256)):
        total = None
        for h in range(4):
            columns = [blocks_ref[4 * h + n, first : first + rows, :] for n in range(4)]
            right = jnp.concatenate(columns, axis=1)
            if first == 0:
                part = lax.dot_general(
                    cov_ref[h * 352 : (h + 1) * 352, :],
                    right,
                    (((0,), (0,)), ((), ())),
                    preferred_element_type=F32,
                )
            else:
                left = jnp.concatenate([diag_ref[2 * h], diag_ref[2 * h + 1]], axis=1)
                part = jnp.dot(left, right, preferred_element_type=F32)
            total = part if total is None else total + part
        for n in range(4):
            tile = total[:, n * 128 : (n + 1) * 128].astype(out_ref.dtype)
            out_ref[n, first : first + rows, :] = tile


def last_kernel(factor_ref, image_ref, out_ref):
    for x in range(4):
        total = None
        for y in range(4):
            n = (y * 4 + x) * 2
            left = jnp.concatenate([factor_ref[n], factor_ref[n + 1]], axis=1)
            part = lax.dot_general(
                left, image_ref[y], (((0,), (0,)), ((), ())), preferred_element_type=F32
            )
            total = part if total is None else total + part
        out_ref[x] = total.astype(out_ref.dtype)


def shift(value, by):
    return lax.ppermute(value, Z, [(i, (i + by) % 16) for i in range(16)])


def swap(value, first, second):
    pairs = [(a * 4 + b, b * 4 + a) for a in range(4) for b in range(4)]
    return lax.ppermute(value, (first, second), pairs)


def exchange(value, axis):
    return lax.all_to_all(value, axis, split_axis=0, concat_axis=0, tiled=True)


def after(value, *others):
    return lax.optimization_barrier((value, *others))[0]


def per_device(
    ancestor_cov,
    ancestor_pattern,
    parent_panel,
    parent_inverse,
    child_pattern,
    child_panel,
    child_inverse,
):
    z = lax.axis_index(Z)
    zl = lax.axis_index("zl")
    column = lax.axis_index(PLANE)

    slab = lax.dynamic_slice_in_dim(parent_panel, column * 128, 128, 1)
    swapped = swap(jnp.concatenate([slab, child_panel], axis=0), "zl", "x")

    ancestor_keep = block_keep(ancestor_pattern, z * 352, 352, 5632)
    column_keep = block_keep(ancestor_pattern, column * 176, 176, 5632)
    child_keep = block_keep(child_pattern, z * 256, 256, 4096)
    child_column_keep = block_keep(child_pattern, column * 128, 128, 4096)
    cov = ancestor_cov * ancestor_keep[:, None].astype(BF) * column_keep[None, :].astype(BF)
    cov = cov.T

    classes = jnp.stack([(zl + 1) % 4, (zl + 3) % 4, (zl + 2) % 4, zl]).astype(jnp.int32)
    bundle = jax.ShapeDtypeStruct((4, 176, 256), BF)
    own, right, left, far = call(
        image_kernel,
        [jax.ShapeDtypeStruct((4, 176, 256), F32), bundle, bundle, bundle],
        [classes, cov, parent_panel],
        2 * 176 * 352 * 4096,
    )
    blocks = lax.all_gather(after(swapped, own), Z, axis=0)
    right, left = shift(right, 1), shift(left, -1)
    far = jnp.concatenate([shift(far[:2], 2), shift(far[2:], -2)], axis=0)
    image = own + right.astype(F32) + left.astype(F32) + far.astype(F32)
    image = image.astype(BF)

    factor = swap(after(child_panel, image), "zh", "y")
    cov_wide = lax.all_gather(after(cov, image), ("y", "c"), axis=0, tiled=True)
    image = after(exchange(image, "zh"), cov_wide)
    image = jnp.sum(image.astype(F32), axis=0).astype(BF)
    factor = lax.all_gather(after(factor, image), PLANE, axis=0)
    image_wide = lax.all_gather(image, ("y", "c"), axis=0, tiled=True)

    (inner,) = call(
        panel_kernel,
        [jax.ShapeDtypeStruct((4, 256, 128), BF)],
        [image_wide, blocks],
        2 * 1408 * 256 * 512,
    )
    inner = jnp.sum(exchange(inner, "x").astype(F32), axis=0)
    parent_diag = (parent_inverse.astype(F32) + inner).astype(BF)

    diag_wide = parent_diag * child_column_keep[None, :].astype(BF)
    diag_wide = lax.all_gather(diag_wide, ("y", "c"), axis=0)
    (product,) = call(
        products_kernel,
        [jax.ShapeDtypeStruct((4, 608, 128), BF)],
        [cov_wide, diag_wide, blocks],
        2 * (1408 * 352 + 1024 * 256) * 512,
    )
    product = -jnp.sum(exchange(product, "x").astype(F32), axis=0)
    ancestor_block = (product[:352] * ancestor_keep[:, None].astype(F32)).astype(BF)
    parent_child = (product[352:] * child_keep[:, None].astype(F32)).astype(BF)

    child_wide = lax.all_gather(parent_child, "zh", axis=0)
    (inner,) = call(
        last_kernel,
        [jax.ShapeDtypeStruct((4, 256, 128), BF)],
        [factor, child_wide],
        2 * 1024 * 1024 * 128,
    )
    inner = jnp.sum(exchange(inner, "zl").astype(F32), axis=0)
    child_diag = (child_inverse.astype(F32) - inner).astype(BF)
    return (ancestor_block, parent_diag, parent_child, child_diag)


def solution(mesh):
    fine = Mesh(mesh.devices.reshape(4, 4, 4, 4, 2), ("zh", "zl", "y", "x", "c"))
    blocked = P(Z, PLANE)
    return jax.shard_map(
        per_device,
        mesh=fine,
        in_specs=(blocked, P(), P(Z, None), blocked, P(), blocked, blocked),
        out_specs=(blocked, blocked, blocked, blocked),
        check_vma=False,
    )
```

```python
import jax
import jax.numpy as jnp
from jax import lax
from jax.experimental import pallas as pl
from jax.experimental.pallas import tpu as pltpu
from jax.sharding import Mesh, PartitionSpec as P

BF = jnp.bfloat16
F32 = jnp.float32
VMEM = pl.BlockSpec(memory_space=pltpu.VMEM)
SMEM = pl.BlockSpec(memory_space=pltpu.SMEM)
Z = ("zh", "zl")
PLANE = ("y", "x", "c")


def block_keep(pattern, first_row, count, total_rows):
    block_rows = total_rows // pattern.shape[0]
    row_ids = first_row + lax.iota(jnp.int32, count)
    block_ids = lax.iota(jnp.int32, pattern.shape[0])
    matches = row_ids[:, None] // block_rows == block_ids[None, :]
    return jnp.sum(jnp.where(matches, pattern[None, :], 0), axis=1)


def call(kernel, outs, args, flops):
    specs = [SMEM if a.dtype == jnp.int32 else VMEM for a in args]
    size = sum(a.size * a.dtype.itemsize for a in args)
    size += sum(o.size * o.dtype.itemsize for o in outs)
    return pl.pallas_call(
        kernel,
        out_shape=outs,
        in_specs=specs,
        out_specs=[VMEM] * len(outs),
        compiler_params=pltpu.CompilerParams(vmem_limit_bytes=20 * 1024 * 1024),
        cost_estimate=pl.CostEstimate(flops=flops, bytes_accessed=size, transcendentals=0),
    )(*args)


def image_kernel(classes, at_ref, panel_ref, own_ref, right_ref, left_ref, far_ref):
    at = at_ref[...]
    for n, out in enumerate((right_ref, left_ref, far_ref, own_ref)):
        for rh in range(4):
            start = pl.multiple_of((4 * rh + classes[n]) * 256, 256)
            block = jnp.dot(at, panel_ref[:, pl.ds(start, 256)], preferred_element_type=F32)
            out[rh] = block.astype(out.dtype)


def block_of(x, h, n):
    over = lax.rem(x - n + 6, 4) - 2 + n - x
    return lax.rem(4 * h - over + 16, 16) + n


def panel_kernel(x_ref, left_ref, blocks_ref, out_ref):
    rows = left_ref.shape[0] // 4
    total = None
    for h in range(4):
        blocks = [blocks_ref[block_of(x_ref[0], h, n), 0:352, :] for n in range(4)]
        part = lax.dot_general(
            left_ref[h * rows : (h + 1) * rows, :],
            jnp.concatenate(blocks, axis=1),
            (((0,), (0,)), ((), ())),
            preferred_element_type=F32,
        )
        total = part if total is None else total + part
    for n in range(4):
        out_ref[n] = total[:, n * 128 : (n + 1) * 128].astype(out_ref.dtype)


def child_kernel(x_ref, left_ref, beside_ref, blocks_ref, out_ref):
    total = None
    for h in range(4):
        blocks = [blocks_ref[block_of(x_ref[0], h, n), 352:608, :] for n in range(4)]
        left = jnp.concatenate([left_ref[2 * h], left_ref[2 * h + 1]], axis=1)
        part = jnp.dot(left, jnp.concatenate(blocks, axis=1), preferred_element_type=F32)
        total = part if total is None else total + part
    for n in range(4):
        out_ref[n, 0:352, :] = beside_ref[n]
        tile = total[:, n * 128 : (n + 1) * 128].astype(out_ref.dtype)
        out_ref[n, 352:608, :] = tile


def last_kernel(factor_ref, image_ref, out_ref):
    for x in range(4):
        total = None
        for y in range(4):
            n = (y * 4 + x) * 2
            left = jnp.concatenate([factor_ref[n], factor_ref[n + 1]], axis=1)
            part = lax.dot_general(
                left, image_ref[y], (((0,), (0,)), ((), ())), preferred_element_type=F32
            )
            total = part if total is None else total + part
        out_ref[x] = total.astype(out_ref.dtype)


def shift(value, by):
    return lax.ppermute(value, Z, [(i, (i + by) % 16) for i in range(16)])


def swap(value, first, second):
    pairs = [(a * 4 + b, b * 4 + a) for a in range(4) for b in range(4)]
    return lax.ppermute(value, (first, second), pairs)


def nearest(value):
    pairs = []
    for p in range(16):
        for n in range(4):
            plane = (p + (n - p + 1) % 4 - 1) % 16
            pairs.append((p * 4 + n, plane * 4 + p % 4))
    return lax.ppermute(value, ("zh", "zl", "x"), pairs)


def exchange(value, axis):
    return lax.all_to_all(value, axis, split_axis=0, concat_axis=0, tiled=True)


def after(value, *others):
    return lax.optimization_barrier((value, *others))[0]


def per_device(
    ancestor_cov,
    ancestor_pattern,
    parent_panel,
    parent_inverse,
    child_pattern,
    child_panel,
    child_inverse,
):
    z = lax.axis_index(Z)
    zl = lax.axis_index("zl")
    column = lax.axis_index(PLANE)
    place = lax.axis_index("x").astype(jnp.int32)[None]

    slab = lax.dynamic_slice_in_dim(parent_panel, column * 128, 128, 1)
    swapped = nearest(jnp.concatenate([slab, child_panel], axis=0))

    ancestor_keep = block_keep(ancestor_pattern, z * 352, 352, 5632)
    column_keep = block_keep(ancestor_pattern, column * 176, 176, 5632)
    child_keep = block_keep(child_pattern, z * 256, 256, 4096)
    child_column_keep = block_keep(child_pattern, column * 128, 128, 4096)
    cov = ancestor_cov * ancestor_keep[:, None].astype(BF) * column_keep[None, :].astype(BF)
    cov = cov.T

    classes = jnp.stack([(zl + 1) % 4, (zl + 3) % 4, (zl + 2) % 4, zl]).astype(jnp.int32)
    bundle = jax.ShapeDtypeStruct((4, 176, 256), BF)
    own, right, left, far = call(
        image_kernel,
        [jax.ShapeDtypeStruct((4, 176, 256), F32), bundle, bundle, bundle],
        [classes, cov, parent_panel],
        2 * 176 * 352 * 4096,
    )
    blocks = lax.all_gather(after(swapped, own), Z, axis=0)
    right, left = shift(right, 1), shift(left, -1)
    far = jnp.concatenate([shift(far[:2], 2), shift(far[2:], -2)], axis=0)
    image = own + right.astype(F32) + left.astype(F32) + far.astype(F32)
    image = image.astype(BF)

    factor = swap(after(child_panel, image), "zh", "y")
    cov_wide = lax.all_gather(after(cov, image), ("y", "c"), axis=0, tiled=True)
    image = after(exchange(image, "zh"), cov_wide)
    image = jnp.sum(image.astype(F32), axis=0).astype(BF)
    factor = lax.all_gather(after(factor, image), PLANE, axis=0)
    image_wide = lax.all_gather(image, ("y", "c"), axis=0, tiled=True)

    (inner,) = call(
        panel_kernel,
        [jax.ShapeDtypeStruct((4, 256, 128), BF)],
        [place, image_wide, blocks],
        2 * 1408 * 256 * 512,
    )
    (beside,) = call(
        panel_kernel,
        [jax.ShapeDtypeStruct((4, 352, 128), BF)],
        [place, cov_wide, after(blocks, inner)],
        2 * 1408 * 352 * 512,
    )
    inner = jnp.sum(exchange(inner, "x").astype(F32), axis=0)
    parent_diag = (parent_inverse.astype(F32) + inner).astype(BF)

    diag_wide = parent_diag * child_column_keep[None, :].astype(BF)
    diag_wide = lax.all_gather(diag_wide, ("y", "c"), axis=0)
    (product,) = call(
        child_kernel,
        [jax.ShapeDtypeStruct((4, 608, 128), BF)],
        [place, diag_wide, beside, blocks],
        2 * 1024 * 256 * 512,
    )
    product = -jnp.sum(exchange(product, "x").astype(F32), axis=0)
    ancestor_block = (product[:352] * ancestor_keep[:, None].astype(F32)).astype(BF)
    parent_child = (product[352:] * child_keep[:, None].astype(F32)).astype(BF)

    child_wide = lax.all_gather(parent_child, "zh", axis=0)
    (inner,) = call(
        last_kernel,
        [jax.ShapeDtypeStruct((4, 256, 128), BF)],
        [factor, child_wide],
        2 * 1024 * 1024 * 128,
    )
    inner = jnp.sum(exchange(inner, "zl").astype(F32), axis=0)
    child_diag = (child_inverse.astype(F32) - inner).astype(BF)
    return (ancestor_block, parent_diag, parent_child, child_diag)


def solution(mesh):
    fine = Mesh(mesh.devices.reshape(4, 4, 4, 4, 2), ("zh", "zl", "y", "x", "c"))
    blocked = P(Z, PLANE)
    return jax.shard_map(
        per_device,
        mesh=fine,
        in_specs=(blocked, P(), P(Z, None), blocked, P(), blocked, blocked),
        out_specs=(blocked, blocked, blocked, blocked),
        check_vma=False,
    )
```

```python
import jax
import jax.numpy as jnp
from jax import lax
from jax.experimental import pallas as pl
from jax.experimental.pallas import tpu as pltpu
from jax.sharding import Mesh, PartitionSpec as P

BF = jnp.bfloat16
F32 = jnp.float32
VMEM = pl.BlockSpec(memory_space=pltpu.VMEM)
SMEM = pl.BlockSpec(memory_space=pltpu.SMEM)
Z = ("zh", "zl")
PLANE = ("y", "x", "c")


def block_keep(pattern, first_row, count, total_rows):
    block_rows = total_rows // pattern.shape[0]
    row_ids = first_row + lax.iota(jnp.int32, count)
    block_ids = lax.iota(jnp.int32, pattern.shape[0])
    matches = row_ids[:, None] // block_rows == block_ids[None, :]
    return jnp.sum(jnp.where(matches, pattern[None, :], 0), axis=1)


def call(kernel, outs, args, flops):
    specs = [SMEM if a.dtype == jnp.int32 else VMEM for a in args]
    size = sum(a.size * a.dtype.itemsize for a in args)
    size += sum(o.size * o.dtype.itemsize for o in outs)
    return pl.pallas_call(
        kernel,
        out_shape=outs,
        in_specs=specs,
        out_specs=[VMEM] * len(outs),
        compiler_params=pltpu.CompilerParams(vmem_limit_bytes=20 * 1024 * 1024),
        cost_estimate=pl.CostEstimate(flops=flops, bytes_accessed=size, transcendentals=0),
    )(*args)


def image_kernel(classes, at_ref, panel_ref, own_ref, right_ref, left_ref, far_ref):
    at = at_ref[...]
    for n, out in enumerate((right_ref, left_ref, far_ref, own_ref)):
        for rh in range(4):
            start = pl.multiple_of((4 * rh + classes[n]) * 256, 256)
            block = jnp.dot(at, panel_ref[:, pl.ds(start, 256)], preferred_element_type=F32)
            out[rh] = block.astype(out.dtype)


def block_of(x, h, n):
    over = lax.rem(x - n + 6, 4) - 2 + n - x
    return lax.rem(4 * h - over + 16, 16) + n


def panel_kernel(x_ref, left_ref, blocks_ref, out_ref):
    rows = left_ref.shape[0] // 4
    total = None
    for h in range(4):
        blocks = [blocks_ref[block_of(x_ref[0], h, n), 0:352, :] for n in range(4)]
        part = lax.dot_general(
            left_ref[h * rows : (h + 1) * rows, :],
            jnp.concatenate(blocks, axis=1),
            (((0,), (0,)), ((), ())),
            preferred_element_type=F32,
        )
        total = part if total is None else total + part
    for n in range(4):
        out_ref[n] = total[:, n * 128 : (n + 1) * 128].astype(out_ref.dtype)


def child_kernel(x_ref, left_ref, beside_ref, blocks_ref, out_ref):
    total = None
    for h in range(4):
        blocks = [blocks_ref[block_of(x_ref[0], h, n), 352:608, :] for n in range(4)]
        left = jnp.concatenate([left_ref[2 * h], left_ref[2 * h + 1]], axis=1)
        part = jnp.dot(left, jnp.concatenate(blocks, axis=1), preferred_element_type=F32)
        total = part if total is None else total + part
    for n in range(4):
        out_ref[n, 0:352, :] = beside_ref[n]
        tile = total[:, n * 128 : (n + 1) * 128].astype(out_ref.dtype)
        out_ref[n, 352:608, :] = tile


def last_kernel(factor_ref, image_ref, out_ref):
    for x in range(4):
        total = None
        for y in range(4):
            n = (y * 4 + x) * 2
            left = jnp.concatenate([factor_ref[n], factor_ref[n + 1]], axis=1)
            part = lax.dot_general(
                left, image_ref[y], (((0,), (0,)), ((), ())), preferred_element_type=F32
            )
            total = part if total is None else total + part
        out_ref[x] = total.astype(out_ref.dtype)


def shift(value, by):
    return lax.ppermute(value, Z, [(i, (i + by) % 16) for i in range(16)])


def swap(value, first, second):
    pairs = [(a * 4 + b, b * 4 + a) for a in range(4) for b in range(4)]
    return lax.ppermute(value, (first, second), pairs)


def nearest(value):
    pairs = []
    for p in range(16):
        for n in range(4):
            plane = (p + (n - p + 1) % 4 - 1) % 16
            pairs.append((p * 4 + n, plane * 4 + p % 4))
    return lax.ppermute(value, ("zh", "zl", "x"), pairs)


def exchange(value, axis):
    return lax.all_to_all(value, axis, split_axis=0, concat_axis=0, tiled=True)


def after(value, *others):
    return lax.optimization_barrier((value, *others))[0]


def per_device(
    ancestor_cov,
    ancestor_pattern,
    parent_panel,
    parent_inverse,
    child_pattern,
    child_panel,
    child_inverse,
):
    z = lax.axis_index(Z)
    zl = lax.axis_index("zl")
    column = lax.axis_index(PLANE)
    place = lax.axis_index("x").astype(jnp.int32)[None]

    slab = lax.dynamic_slice_in_dim(parent_panel, column * 128, 128, 1)
    swapped = nearest(jnp.concatenate([slab, child_panel], axis=0))

    ancestor_keep = block_keep(ancestor_pattern, z * 352, 352, 5632)
    column_keep = block_keep(ancestor_pattern, column * 176, 176, 5632)
    child_keep = block_keep(child_pattern, z * 256, 256, 4096)
    child_column_keep = block_keep(child_pattern, column * 128, 128, 4096)
    cov = ancestor_cov * ancestor_keep[:, None].astype(BF) * column_keep[None, :].astype(BF)
    cov = cov.T

    classes = jnp.stack([(zl + 1) % 4, (zl + 3) % 4, (zl + 2) % 4, zl]).astype(jnp.int32)
    bundle = jax.ShapeDtypeStruct((4, 176, 256), BF)
    own, right, left, far = call(
        image_kernel,
        [jax.ShapeDtypeStruct((4, 176, 256), F32), bundle, bundle, bundle],
        [classes, cov, parent_panel],
        2 * 176 * 352 * 4096,
    )
    blocks = lax.all_gather(after(swapped, own), Z, axis=0)
    right, left = shift(right, 1), shift(left, -1)
    far = jnp.concatenate([shift(far[:2], 2), shift(far[2:], -2)], axis=0)
    image = own + right.astype(F32) + left.astype(F32) + far.astype(F32)
    image = image.astype(BF)

    cov_wide = lax.all_gather(after(cov, image), ("y", "c"), axis=0, tiled=True)
    image = after(exchange(image, "zh"), cov_wide)
    image = jnp.sum(image.astype(F32), axis=0).astype(BF)
    factor = swap(after(child_panel, image), "zh", "y")
    image_wide = lax.all_gather(image, ("y", "c"), axis=0, tiled=True)
    factor = lax.all_gather(after(factor, image_wide), PLANE, axis=0)

    (inner,) = call(
        panel_kernel,
        [jax.ShapeDtypeStruct((4, 256, 128), BF)],
        [place, image_wide, blocks],
        2 * 1408 * 256 * 512,
    )
    (beside,) = call(
        panel_kernel,
        [jax.ShapeDtypeStruct((4, 352, 128), BF)],
        [place, cov_wide, after(blocks, inner)],
        2 * 1408 * 352 * 512,
    )
    inner = jnp.sum(exchange(inner, "x").astype(F32), axis=0)
    parent_diag = (parent_inverse.astype(F32) + inner).astype(BF)

    diag_wide = parent_diag * child_column_keep[None, :].astype(BF)
    diag_wide = lax.all_gather(diag_wide, ("y", "c"), axis=0)
    (product,) = call(
        child_kernel,
        [jax.ShapeDtypeStruct((4, 608, 128), BF)],
        [place, diag_wide, beside, blocks],
        2 * 1024 * 256 * 512,
    )
    product = -jnp.sum(exchange(product, "x").astype(F32), axis=0)
    ancestor_block = (product[:352] * ancestor_keep[:, None].astype(F32)).astype(BF)
    parent_child = (product[352:] * child_keep[:, None].astype(F32)).astype(BF)

    child_wide = lax.all_gather(parent_child, "zh", axis=0)
    (inner,) = call(
        last_kernel,
        [jax.ShapeDtypeStruct((4, 256, 128), BF)],
        [factor, child_wide],
        2 * 1024 * 1024 * 128,
    )
    inner = jnp.sum(exchange(inner, "zl").astype(F32), axis=0)
    child_diag = (child_inverse.astype(F32) - inner).astype(BF)
    return (ancestor_block, parent_diag, parent_child, child_diag)


def solution(mesh):
    fine = Mesh(mesh.devices.reshape(4, 4, 4, 4, 2), ("zh", "zl", "y", "x", "c"))
    blocked = P(Z, PLANE)
    return jax.shard_map(
        per_device,
        mesh=fine,
        in_specs=(blocked, P(), P(Z, None), blocked, P(), blocked, blocked),
        out_specs=(blocked, blocked, blocked, blocked),
        check_vma=False,
    )
```

```python
import jax
import jax.numpy as jnp
from jax import lax
from jax.experimental import pallas as pl
from jax.experimental.pallas import tpu as pltpu
from jax.sharding import Mesh, PartitionSpec as P

BF = jnp.bfloat16
F32 = jnp.float32
VMEM = pl.BlockSpec(memory_space=pltpu.VMEM)
SMEM = pl.BlockSpec(memory_space=pltpu.SMEM)
Z = ("zh", "zl")
PLANE = ("y", "x", "c")


def block_keep(pattern, first_row, count, total_rows):
    block_rows = total_rows // pattern.shape[0]
    row_ids = first_row + lax.iota(jnp.int32, count)
    block_ids = lax.iota(jnp.int32, pattern.shape[0])
    matches = row_ids[:, None] // block_rows == block_ids[None, :]
    return jnp.sum(jnp.where(matches, pattern[None, :], 0), axis=1)


def call(kernel, outs, args, flops):
    specs = [SMEM if a.dtype == jnp.int32 else VMEM for a in args]
    size = sum(a.size * a.dtype.itemsize for a in args)
    size += sum(o.size * o.dtype.itemsize for o in outs)
    return pl.pallas_call(
        kernel,
        out_shape=outs,
        in_specs=specs,
        out_specs=[VMEM] * len(outs),
        compiler_params=pltpu.CompilerParams(vmem_limit_bytes=20 * 1024 * 1024),
        cost_estimate=pl.CostEstimate(flops=flops, bytes_accessed=size, transcendentals=0),
    )(*args)


def image_kernel(classes, at_ref, panel_ref, own_ref, right_ref, left_ref, far_ref):
    at = at_ref[...]
    for n, out in enumerate((right_ref, left_ref, far_ref, own_ref)):
        for rh in range(4):
            start = pl.multiple_of((4 * rh + classes[n]) * 256, 256)
            block = jnp.dot(at, panel_ref[:, pl.ds(start, 256)], preferred_element_type=F32)
            out[rh] = block.astype(out.dtype)


def block_of(x, h, n):
    over = lax.rem(x - n + 6, 4) - 2 + n - x
    return lax.rem(4 * h - over + 16, 16) + n


def panel_kernel(x_ref, left_ref, blocks_ref, out_ref):
    rows = left_ref.shape[0] // 4
    total = None
    for h in range(4):
        blocks = [blocks_ref[block_of(x_ref[0], h, n), 0:352, :] for n in range(4)]
        part = lax.dot_general(
            left_ref[h * rows : (h + 1) * rows, :],
            jnp.concatenate(blocks, axis=1),
            (((0,), (0,)), ((), ())),
            preferred_element_type=F32,
        )
        total = part if total is None else total + part
    for n in range(4):
        out_ref[n] = total[:, n * 128 : (n + 1) * 128].astype(out_ref.dtype)


def beside_kernel(x_ref, left_ref, blocks_ref, *outs):
    bands = [lax.rem(x_ref[0] + d, 4) for d in range(4)]
    total = None
    for h in range(4):
        blocks = [blocks_ref[block_of(x_ref[0], h, n), 0:352, :] for n in bands]
        part = lax.dot_general(
            left_ref[h * 352 : (h + 1) * 352, :],
            jnp.concatenate(blocks, axis=1),
            (((0,), (0,)), ((), ())),
            preferred_element_type=F32,
        )
        total = part if total is None else total + part
    for n, out in enumerate(outs):
        out[...] = total[:, n * 128 : (n + 1) * 128].astype(out.dtype)


def child_kernel(x_ref, left_ref, blocks_ref, out_ref):
    total = None
    for h in range(4):
        blocks = [blocks_ref[block_of(x_ref[0], h, n), 352:608, :] for n in range(4)]
        left = jnp.concatenate([left_ref[2 * h], left_ref[2 * h + 1]], axis=1)
        part = jnp.dot(left, jnp.concatenate(blocks, axis=1), preferred_element_type=F32)
        total = part if total is None else total + part
    for n in range(4):
        out_ref[n] = total[:, n * 128 : (n + 1) * 128].astype(out_ref.dtype)


def last_kernel(factor_ref, image_ref, out_ref):
    for x in range(4):
        total = None
        for y in range(4):
            n = (y * 4 + x) * 2
            left = jnp.concatenate([factor_ref[n], factor_ref[n + 1]], axis=1)
            part = lax.dot_general(
                left, image_ref[y], (((0,), (0,)), ((), ())), preferred_element_type=F32
            )
            total = part if total is None else total + part
        out_ref[x] = total.astype(out_ref.dtype)


def shift(value, by):
    return lax.ppermute(value, Z, [(i, (i + by) % 16) for i in range(16)])


def along_x(value, by):
    return lax.ppermute(value, "x", [(i, (i + by) % 4) for i in range(4)])


def swap(value, first, second):
    pairs = [(a * 4 + b, b * 4 + a) for a in range(4) for b in range(4)]
    return lax.ppermute(value, (first, second), pairs)


def nearest(value):
    pairs = []
    for p in range(16):
        for n in range(4):
            plane = (p + (n - p + 1) % 4 - 1) % 16
            pairs.append((p * 4 + n, plane * 4 + p % 4))
    return lax.ppermute(value, ("zh", "zl", "x"), pairs)


def exchange(value, axis):
    return lax.all_to_all(value, axis, split_axis=0, concat_axis=0, tiled=True)


def after(value, *others):
    return lax.optimization_barrier((value, *others))[0]


def per_device(
    ancestor_cov,
    ancestor_pattern,
    parent_panel,
    parent_inverse,
    child_pattern,
    child_panel,
    child_inverse,
):
    z = lax.axis_index(Z)
    zl = lax.axis_index("zl")
    column = lax.axis_index(PLANE)
    place = lax.axis_index("x").astype(jnp.int32)[None]

    slab = lax.dynamic_slice_in_dim(parent_panel, column * 128, 128, 1)
    swapped = nearest(jnp.concatenate([slab, child_panel], axis=0))

    ancestor_keep = block_keep(ancestor_pattern, z * 352, 352, 5632)
    column_keep = block_keep(ancestor_pattern, column * 176, 176, 5632)
    child_keep = block_keep(child_pattern, z * 256, 256, 4096)
    child_column_keep = block_keep(child_pattern, column * 128, 128, 4096)
    cov = ancestor_cov * ancestor_keep[:, None].astype(BF) * column_keep[None, :].astype(BF)
    cov = cov.T

    classes = jnp.stack([(zl + 1) % 4, (zl + 3) % 4, (zl + 2) % 4, zl]).astype(jnp.int32)
    bundle = jax.ShapeDtypeStruct((4, 176, 256), BF)
    own, right, left, far = call(
        image_kernel,
        [jax.ShapeDtypeStruct((4, 176, 256), F32), bundle, bundle, bundle],
        [classes, cov, parent_panel],
        2 * 176 * 352 * 4096,
    )
    blocks = lax.all_gather(after(swapped, own), Z, axis=0)
    right, left = shift(right, 1), shift(left, -1)
    far = jnp.concatenate([shift(far[:2], 2), shift(far[2:], -2)], axis=0)
    image = own + right.astype(F32) + left.astype(F32) + far.astype(F32)
    image = image.astype(BF)

    cov_wide = lax.all_gather(after(cov, image), ("y", "c"), axis=0, tiled=True)
    image = after(exchange(image, "zh"), cov_wide)
    image = jnp.sum(image.astype(F32), axis=0).astype(BF)
    factor = swap(after(child_panel, image), "zh", "y")
    image_wide = lax.all_gather(image, ("y", "c"), axis=0, tiled=True)
    factor = lax.all_gather(after(factor, image_wide), PLANE, axis=0)

    (inner,) = call(
        panel_kernel,
        [jax.ShapeDtypeStruct((4, 256, 128), BF)],
        [place, image_wide, blocks],
        2 * 1408 * 256 * 512,
    )
    part = jax.ShapeDtypeStruct((352, 128), BF)
    besides = call(
        beside_kernel,
        [jax.ShapeDtypeStruct((352, 128), F32), part, part, part],
        [place, cov_wide, after(blocks, inner)],
        2 * 1408 * 352 * 512,
    )
    inner = jnp.sum(after(exchange(inner, "x"), besides[0]).astype(F32), axis=0)
    parent_diag = (parent_inverse.astype(F32) + inner).astype(BF)

    diag_wide = parent_diag * child_column_keep[None, :].astype(BF)
    diag_wide = lax.all_gather(diag_wide, ("y", "c"), axis=0)
    (product,) = call(
        child_kernel,
        [jax.ShapeDtypeStruct((4, 256, 128), BF)],
        [place, diag_wide, blocks],
        2 * 1024 * 256 * 512,
    )
    moved = [along_x(after(besides[d], product), d) for d in range(1, 4)]
    product = jnp.sum(exchange(product, "x").astype(F32), axis=0)
    parent_child = (-product * child_keep[:, None].astype(F32)).astype(BF)

    child_wide = lax.all_gather(parent_child, "zh", axis=0)
    (inner,) = call(
        last_kernel,
        [jax.ShapeDtypeStruct((4, 256, 128), BF)],
        [factor, after(child_wide, *moved)],
        2 * 1024 * 1024 * 128,
    )
    inner = jnp.sum(exchange(inner, "zl").astype(F32), axis=0)
    product = besides[0] + sum(block.astype(F32) for block in moved)
    ancestor_block = (-product * ancestor_keep[:, None].astype(F32)).astype(BF)
    child_diag = (child_inverse.astype(F32) - inner).astype(BF)
    return (ancestor_block, parent_diag, parent_child, child_diag)


def solution(mesh):
    fine = Mesh(mesh.devices.reshape(4, 4, 4, 4, 2), ("zh", "zl", "y", "x", "c"))
    blocked = P(Z, PLANE)
    return jax.shard_map(
        per_device,
        mesh=fine,
        in_specs=(blocked, P(), P(Z, None), blocked, P(), blocked, blocked),
        out_specs=(blocked, blocked, blocked, blocked),
        check_vma=False,
    )
```

```python
import jax
import jax.numpy as jnp
from jax import lax
from jax.experimental import pallas as pl
from jax.experimental.pallas import tpu as pltpu
from jax.sharding import Mesh, PartitionSpec as P

BF = jnp.bfloat16
F32 = jnp.float32
VMEM = pl.BlockSpec(memory_space=pltpu.VMEM)
SMEM = pl.BlockSpec(memory_space=pltpu.SMEM)
Z = ("zh", "zl")
PLANE = ("y", "x", "c")


def block_keep(pattern, first_row, count, total_rows):
    block_rows = total_rows // pattern.shape[0]
    row_ids = first_row + lax.iota(jnp.int32, count)
    block_ids = lax.iota(jnp.int32, pattern.shape[0])
    matches = row_ids[:, None] // block_rows == block_ids[None, :]
    return jnp.sum(jnp.where(matches, pattern[None, :], 0), axis=1)


def call(kernel, outs, args, flops):
    specs = [SMEM if a.dtype == jnp.int32 else VMEM for a in args]
    size = sum(a.size * a.dtype.itemsize for a in args)
    size += sum(o.size * o.dtype.itemsize for o in outs)
    return pl.pallas_call(
        kernel,
        out_shape=outs,
        in_specs=specs,
        out_specs=[VMEM] * len(outs),
        compiler_params=pltpu.CompilerParams(vmem_limit_bytes=20 * 1024 * 1024),
        cost_estimate=pl.CostEstimate(flops=flops, bytes_accessed=size, transcendentals=0),
    )(*args)


def image_kernel(classes, at_ref, panel_ref, own_ref, right_ref, left_ref, far_ref):
    at = at_ref[...]
    for n, out in enumerate((right_ref, left_ref, far_ref, own_ref)):
        for rh in range(4):
            start = pl.multiple_of((4 * rh + classes[n]) * 256, 256)
            block = jnp.dot(at, panel_ref[:, pl.ds(start, 256)], preferred_element_type=F32)
            out[rh] = block.astype(out.dtype)


def block_of(x, h, n):
    over = lax.rem(x - n + 6, 4) - 2 + n - x
    return lax.rem(4 * h - over + 16, 16) + n


def panel_kernel(x_ref, left_ref, blocks_ref, out_ref):
    rows = left_ref.shape[0] // 4
    total = None
    for h in range(4):
        blocks = [blocks_ref[block_of(x_ref[0], h, n), 0:352, :] for n in range(4)]
        part = lax.dot_general(
            left_ref[h * rows : (h + 1) * rows, :],
            jnp.concatenate(blocks, axis=1),
            (((0,), (0,)), ((), ())),
            preferred_element_type=F32,
        )
        total = part if total is None else total + part
    for n in range(4):
        out_ref[n] = total[:, n * 128 : (n + 1) * 128].astype(out_ref.dtype)


def beside_kernel(x_ref, left_ref, blocks_ref, *outs):
    bands = [lax.rem(x_ref[0] + d, 4) for d in range(4)]
    total = None
    for h in range(4):
        blocks = [blocks_ref[block_of(x_ref[0], h, n), 0:352, :] for n in bands]
        part = lax.dot_general(
            left_ref[h * 352 : (h + 1) * 352, :],
            jnp.concatenate(blocks, axis=1),
            (((0,), (0,)), ((), ())),
            preferred_element_type=F32,
        )
        total = part if total is None else total + part
    for n, out in enumerate(outs):
        out[...] = total[:, n * 128 : (n + 1) * 128].astype(out.dtype)


def child_kernel(x_ref, left_ref, blocks_ref, out_ref):
    total = None
    for h in range(4):
        blocks = [blocks_ref[block_of(x_ref[0], h, n), 352:608, :] for n in range(4)]
        left = jnp.concatenate([left_ref[2 * h], left_ref[2 * h + 1]], axis=1)
        part = jnp.dot(left, jnp.concatenate(blocks, axis=1), preferred_element_type=F32)
        total = part if total is None else total + part
    for n in range(4):
        out_ref[n] = total[:, n * 128 : (n + 1) * 128].astype(out_ref.dtype)


def last_kernel(factor_ref, image_ref, out_ref):
    for x in range(4):
        total = None
        for y in range(4):
            n = (y * 4 + x) * 2
            left = jnp.concatenate([factor_ref[n], factor_ref[n + 1]], axis=1)
            part = lax.dot_general(
                left, image_ref[y], (((0,), (0,)), ((), ())), preferred_element_type=F32
            )
            total = part if total is None else total + part
        out_ref[x] = total.astype(out_ref.dtype)


def shift(value, by):
    return lax.ppermute(value, Z, [(i, (i + by) % 16) for i in range(16)])


def along_x(value, by):
    return lax.ppermute(value, "x", [(i, (i + by) % 4) for i in range(4)])


def swap(value, first, second):
    pairs = [(a * 4 + b, b * 4 + a) for a in range(4) for b in range(4)]
    return lax.ppermute(value, (first, second), pairs)


def nearest(value):
    pairs = []
    for p in range(16):
        for n in range(4):
            plane = (p + (n - p + 1) % 4 - 1) % 16
            pairs.append((p * 4 + n, plane * 4 + p % 4))
    return lax.ppermute(value, ("zh", "zl", "x"), pairs)


def exchange(value, axis):
    return lax.all_to_all(value, axis, split_axis=0, concat_axis=0, tiled=True)


def after(value, *others):
    return lax.optimization_barrier((value, *others))[0]


def per_device(
    ancestor_cov,
    ancestor_pattern,
    parent_panel,
    parent_inverse,
    child_pattern,
    child_panel,
    child_inverse,
):
    z = lax.axis_index(Z)
    zl = lax.axis_index("zl")
    column = lax.axis_index(PLANE)
    place = lax.axis_index("x").astype(jnp.int32)[None]

    slab = lax.dynamic_slice_in_dim(parent_panel, column * 128, 128, 1)
    swapped = nearest(jnp.concatenate([slab, child_panel], axis=0))

    ancestor_keep = block_keep(ancestor_pattern, z * 352, 352, 5632)
    column_keep = block_keep(ancestor_pattern, column * 176, 176, 5632)
    child_keep = block_keep(child_pattern, z * 256, 256, 4096)
    child_column_keep = block_keep(child_pattern, column * 128, 128, 4096)
    cov = ancestor_cov * ancestor_keep[:, None].astype(BF) * column_keep[None, :].astype(BF)
    cov = cov.T

    classes = jnp.stack([(zl + 1) % 4, (zl + 3) % 4, (zl + 2) % 4, zl]).astype(jnp.int32)
    bundle = jax.ShapeDtypeStruct((4, 176, 256), BF)
    own, right, left, far = call(
        image_kernel,
        [jax.ShapeDtypeStruct((4, 176, 256), F32), bundle, bundle, bundle],
        [classes, cov, parent_panel],
        2 * 176 * 352 * 4096,
    )
    blocks = lax.all_gather(after(swapped, own), Z, axis=0)
    right, left = shift(right, 1), shift(left, -1)
    far = jnp.concatenate([shift(far[:2], 2), shift(far[2:], -2)], axis=0)
    image = own + right.astype(F32) + left.astype(F32) + far.astype(F32)
    image = image.astype(BF)

    cov_wide = lax.all_gather(after(cov, image), ("y", "c"), axis=0, tiled=True)
    image = after(exchange(image, "zh"), cov_wide)
    image = jnp.sum(image.astype(F32), axis=0).astype(BF)
    factor = swap(after(child_panel, image), "zh", "y")
    image_wide = lax.all_gather(image, ("y", "c"), axis=0, tiled=True)
    factor = lax.all_gather(after(factor, image_wide), PLANE, axis=0)

    (inner,) = call(
        panel_kernel,
        [jax.ShapeDtypeStruct((4, 256, 128), BF)],
        [place, image_wide, blocks],
        2 * 1408 * 256 * 512,
    )
    part = jax.ShapeDtypeStruct((352, 128), BF)
    besides = call(
        beside_kernel,
        [jax.ShapeDtypeStruct((352, 128), F32), part, part, part],
        [place, cov_wide, after(blocks, inner)],
        2 * 1408 * 352 * 512,
    )
    inner = jnp.sum(after(exchange(inner, "x"), besides[0]).astype(F32), axis=0)
    parent_diag = (parent_inverse.astype(F32) + inner).astype(BF)

    across = along_x(besides[2], 2)
    diag_wide = parent_diag * child_column_keep[None, :].astype(BF)
    diag_wide = lax.all_gather(diag_wide, ("y", "c"), axis=0)
    (product,) = call(
        child_kernel,
        [jax.ShapeDtypeStruct((4, 256, 128), BF)],
        [place, after(diag_wide, across), blocks],
        2 * 1024 * 256 * 512,
    )
    moved = [along_x(after(besides[d], product), d) for d in (1, 3)] + [across]
    product = jnp.sum(exchange(product, "x").astype(F32), axis=0)
    parent_child = (-product * child_keep[:, None].astype(F32)).astype(BF)

    child_wide = lax.all_gather(parent_child, "zh", axis=0)
    (inner,) = call(
        last_kernel,
        [jax.ShapeDtypeStruct((4, 256, 128), BF)],
        [factor, after(child_wide, *moved)],
        2 * 1024 * 1024 * 128,
    )
    inner = jnp.sum(exchange(inner, "zl").astype(F32), axis=0)
    product = besides[0] + sum(block.astype(F32) for block in moved)
    ancestor_block = (-product * ancestor_keep[:, None].astype(F32)).astype(BF)
    child_diag = (child_inverse.astype(F32) - inner).astype(BF)
    return (ancestor_block, parent_diag, parent_child, child_diag)


def solution(mesh):
    fine = Mesh(mesh.devices.reshape(4, 4, 4, 4, 2), ("zh", "zl", "y", "x", "c"))
    blocked = P(Z, PLANE)
    return jax.shard_map(
        per_device,
        mesh=fine,
        in_specs=(blocked, P(), P(Z, None), blocked, P(), blocked, blocked),
        out_specs=(blocked, blocked, blocked, blocked),
        check_vma=False,
    )
```

```python
import jax
import jax.numpy as jnp
from jax import lax
from jax.experimental import pallas as pl
from jax.experimental.pallas import tpu as pltpu
from jax.sharding import Mesh, PartitionSpec as P

BF = jnp.bfloat16
F32 = jnp.float32
VMEM = pl.BlockSpec(memory_space=pltpu.VMEM)
SMEM = pl.BlockSpec(memory_space=pltpu.SMEM)
Z = ("zh", "zl")
PLANE = ("y", "x", "c")


def block_keep(pattern, first_row, count, total_rows):
    block_rows = total_rows // pattern.shape[0]
    row_ids = first_row + lax.iota(jnp.int32, count)
    block_ids = lax.iota(jnp.int32, pattern.shape[0])
    matches = row_ids[:, None] // block_rows == block_ids[None, :]
    return jnp.sum(jnp.where(matches, pattern[None, :], 0), axis=1)


def call(kernel, outs, args, flops):
    specs = [SMEM if a.dtype == jnp.int32 else VMEM for a in args]
    size = sum(a.size * a.dtype.itemsize for a in args)
    size += sum(o.size * o.dtype.itemsize for o in outs)
    return pl.pallas_call(
        kernel,
        out_shape=outs,
        in_specs=specs,
        out_specs=[VMEM] * len(outs),
        compiler_params=pltpu.CompilerParams(vmem_limit_bytes=20 * 1024 * 1024),
        cost_estimate=pl.CostEstimate(flops=flops, bytes_accessed=size, transcendentals=0),
    )(*args)


def image_kernel(classes, at_ref, panel_ref, own_ref, right_ref, left_ref, far_ref):
    at = at_ref[...]
    for n, out in enumerate((right_ref, left_ref, far_ref, own_ref)):
        for rh in range(4):
            start = pl.multiple_of((4 * rh + classes[n]) * 256, 256)
            block = jnp.dot(at, panel_ref[:, pl.ds(start, 256)], preferred_element_type=F32)
            out[rh] = block.astype(out.dtype)


def block_of(x, h, n):
    over = lax.rem(x - n + 6, 4) - 2 + n - x
    return lax.rem(4 * h - over + 16, 16) + n


def panel_kernel(x_ref, left_ref, blocks_ref, out_ref):
    rows = left_ref.shape[0] // 4
    total = None
    for h in range(4):
        blocks = [blocks_ref[block_of(x_ref[0], h, n), 0:352, :] for n in range(4)]
        part = lax.dot_general(
            left_ref[h * rows : (h + 1) * rows, :],
            jnp.concatenate(blocks, axis=1),
            (((0,), (0,)), ((), ())),
            preferred_element_type=F32,
        )
        total = part if total is None else total + part
    for n in range(4):
        out_ref[n] = total[:, n * 128 : (n + 1) * 128].astype(out_ref.dtype)


def beside_kernel(x_ref, left_ref, blocks_ref, *outs):
    bands = [lax.rem(x_ref[0] + d, 4) for d in range(4)]
    total = None
    for h in range(4):
        blocks = [blocks_ref[block_of(x_ref[0], h, n), 0:352, :] for n in bands]
        part = lax.dot_general(
            left_ref[h * 352 : (h + 1) * 352, :],
            jnp.concatenate(blocks, axis=1),
            (((0,), (0,)), ((), ())),
            preferred_element_type=F32,
        )
        total = part if total is None else total + part
    for n, out in enumerate(outs):
        out[...] = total[:, n * 128 : (n + 1) * 128].astype(out.dtype)


def child_kernel(x_ref, left_ref, blocks_ref, out_ref):
    total = None
    for h in range(4):
        blocks = [blocks_ref[block_of(x_ref[0], h, n), 352:608, :] for n in range(4)]
        left = jnp.concatenate([left_ref[2 * h], left_ref[2 * h + 1]], axis=1)
        part = jnp.dot(left, jnp.concatenate(blocks, axis=1), preferred_element_type=F32)
        total = part if total is None else total + part
    for n in range(4):
        out_ref[n] = total[:, n * 128 : (n + 1) * 128].astype(out_ref.dtype)


def last_kernel(factor_ref, image_ref, out_ref):
    for x in range(4):
        total = None
        for y in range(4):
            left = jnp.concatenate([factor_ref[y, x, 0], factor_ref[y, x, 1]], axis=1)
            part = lax.dot_general(
                left, image_ref[y], (((0,), (0,)), ((), ())), preferred_element_type=F32
            )
            total = part if total is None else total + part
        out_ref[x] = total.astype(out_ref.dtype)


def shift(value, by):
    return lax.ppermute(value, Z, [(i, (i + by) % 16) for i in range(16)])


def along_x(value, by):
    return lax.ppermute(value, "x", [(i, (i + by) % 4) for i in range(4)])


def swap(value, first, second):
    pairs = [(a * 4 + b, b * 4 + a) for a in range(4) for b in range(4)]
    return lax.ppermute(value, (first, second), pairs)


def nearest(value):
    pairs = []
    for p in range(16):
        for n in range(4):
            plane = (p + (n - p + 1) % 4 - 1) % 16
            pairs.append((p * 4 + n, plane * 4 + p % 4))
    return lax.ppermute(value, ("zh", "zl", "x"), pairs)


def exchange(value, axis):
    return lax.all_to_all(value, axis, split_axis=0, concat_axis=0, tiled=True)


def after(value, *others):
    return lax.optimization_barrier((value, *others))[0]


def per_device(
    ancestor_cov,
    ancestor_pattern,
    parent_panel,
    parent_inverse,
    child_pattern,
    child_panel,
    child_inverse,
):
    z = lax.axis_index(Z)
    zl = lax.axis_index("zl")
    column = lax.axis_index(PLANE)
    place = lax.axis_index("x").astype(jnp.int32)[None]

    slab = lax.dynamic_slice_in_dim(parent_panel, column * 128, 128, 1)
    swapped = nearest(jnp.concatenate([slab, child_panel], axis=0))

    ancestor_keep = block_keep(ancestor_pattern, z * 352, 352, 5632)
    column_keep = block_keep(ancestor_pattern, column * 176, 176, 5632)
    child_keep = block_keep(child_pattern, z * 256, 256, 4096)
    child_column_keep = block_keep(child_pattern, column * 128, 128, 4096)
    cov = ancestor_cov * ancestor_keep[:, None].astype(BF) * column_keep[None, :].astype(BF)
    cov = cov.T

    classes = jnp.stack([(zl + 1) % 4, (zl + 3) % 4, (zl + 2) % 4, zl]).astype(jnp.int32)
    bundle = jax.ShapeDtypeStruct((4, 176, 256), BF)
    own, right, left, far = call(
        image_kernel,
        [jax.ShapeDtypeStruct((4, 176, 256), F32), bundle, bundle, bundle],
        [classes, cov, parent_panel],
        2 * 176 * 352 * 4096,
    )
    blocks = lax.all_gather(after(swapped, own), Z, axis=0)
    right, left = shift(right, 1), shift(left, -1)
    far = jnp.concatenate([shift(far[:2], 2), shift(far[2:], -2)], axis=0)
    image = own + right.astype(F32) + left.astype(F32) + far.astype(F32)
    image = image.astype(BF)

    cov_wide = lax.all_gather(after(cov, image), ("y", "c"), axis=0, tiled=True)
    image = after(exchange(image, "zh"), cov_wide)
    image = jnp.sum(image.astype(F32), axis=0).astype(BF)
    factor = swap(after(child_panel, image), "zh", "y")
    image_wide = lax.all_gather(image, ("y", "c"), axis=0, tiled=True)
    factor = lax.all_gather(after(factor, image_wide), "c", axis=0)
    factor = lax.all_gather(factor, "x", axis=0)
    image_wide = after(image_wide, factor)
    factor = lax.all_gather(factor, "y", axis=0)

    (inner,) = call(
        panel_kernel,
        [jax.ShapeDtypeStruct((4, 256, 128), BF)],
        [place, image_wide, blocks],
        2 * 1408 * 256 * 512,
    )
    part = jax.ShapeDtypeStruct((352, 128), BF)
    besides = call(
        beside_kernel,
        [jax.ShapeDtypeStruct((352, 128), F32), part, part, part],
        [place, cov_wide, after(blocks, inner)],
        2 * 1408 * 352 * 512,
    )
    inner = jnp.sum(after(exchange(inner, "x"), besides[0]).astype(F32), axis=0)
    parent_diag = (parent_inverse.astype(F32) + inner).astype(BF)

    across = along_x(besides[2], 2)
    diag_wide = parent_diag * child_column_keep[None, :].astype(BF)
    diag_wide = lax.all_gather(diag_wide, ("y", "c"), axis=0)
    (product,) = call(
        child_kernel,
        [jax.ShapeDtypeStruct((4, 256, 128), BF)],
        [place, after(diag_wide, across), blocks],
        2 * 1024 * 256 * 512,
    )
    moved = [along_x(after(besides[d], product), d) for d in (1, 3)] + [across]
    product = jnp.sum(exchange(product, "x").astype(F32), axis=0)
    parent_child = (-product * child_keep[:, None].astype(F32)).astype(BF)

    child_wide = lax.all_gather(after(parent_child, factor), "zh", axis=0)
    (inner,) = call(
        last_kernel,
        [jax.ShapeDtypeStruct((4, 256, 128), BF)],
        [factor, after(child_wide, *moved)],
        2 * 1024 * 1024 * 128,
    )
    inner = jnp.sum(exchange(inner, "zl").astype(F32), axis=0)
    product = besides[0] + sum(block.astype(F32) for block in moved)
    ancestor_block = (-product * ancestor_keep[:, None].astype(F32)).astype(BF)
    child_diag = (child_inverse.astype(F32) - inner).astype(BF)
    return (ancestor_block, parent_diag, parent_child, child_diag)


def solution(mesh):
    fine = Mesh(mesh.devices.reshape(4, 4, 4, 4, 2), ("zh", "zl", "y", "x", "c"))
    blocked = P(Z, PLANE)
    return jax.shard_map(
        per_device,
        mesh=fine,
        in_specs=(blocked, P(), P(Z, None), blocked, P(), blocked, blocked),
        out_specs=(blocked, blocked, blocked, blocked),
        check_vma=False,
    )
```

```python
import jax
import jax.numpy as jnp
from jax import lax
from jax.experimental import pallas as pl
from jax.experimental.pallas import tpu as pltpu
from jax.sharding import Mesh, PartitionSpec as P

BF = jnp.bfloat16
F32 = jnp.float32
VMEM = pl.BlockSpec(memory_space=pltpu.VMEM)
SMEM = pl.BlockSpec(memory_space=pltpu.SMEM)
Z = ("zh", "zl")
PLANE = ("y", "x", "c")


def block_keep(pattern, first_row, count, total_rows):
    block_rows = total_rows // pattern.shape[0]
    row_ids = first_row + lax.iota(jnp.int32, count)
    block_ids = lax.iota(jnp.int32, pattern.shape[0])
    matches = row_ids[:, None] // block_rows == block_ids[None, :]
    return jnp.sum(jnp.where(matches, pattern[None, :], 0), axis=1)


def call(kernel, outs, args, flops):
    specs = [SMEM if a.dtype == jnp.int32 else VMEM for a in args]
    size = sum(a.size * a.dtype.itemsize for a in args)
    size += sum(o.size * o.dtype.itemsize for o in outs)
    return pl.pallas_call(
        kernel,
        out_shape=outs,
        in_specs=specs,
        out_specs=[VMEM] * len(outs),
        compiler_params=pltpu.CompilerParams(vmem_limit_bytes=20 * 1024 * 1024),
        cost_estimate=pl.CostEstimate(flops=flops, bytes_accessed=size, transcendentals=0),
    )(*args)


def image_kernel(classes, at_ref, panel_ref, own_ref, right_ref, left_ref, far_ref):
    at = at_ref[...]
    for n, out in enumerate((right_ref, left_ref, far_ref, own_ref)):
        for rh in range(4):
            start = pl.multiple_of((4 * rh + classes[n]) * 256, 256)
            block = jnp.dot(at, panel_ref[:, pl.ds(start, 256)], preferred_element_type=F32)
            out[rh] = block.astype(out.dtype)


def block_of(x, h, n):
    over = lax.rem(x - n + 6, 4) - 2 + n - x
    return lax.rem(4 * h - over + 16, 16) + n


def panel_kernel(x_ref, left_ref, blocks_ref, out_ref):
    rows = left_ref.shape[0] // 4
    total = None
    for h in range(4):
        blocks = [blocks_ref[block_of(x_ref[0], h, n), 0:352, :] for n in range(4)]
        part = lax.dot_general(
            left_ref[h * rows : (h + 1) * rows, :],
            jnp.concatenate(blocks, axis=1),
            (((0,), (0,)), ((), ())),
            preferred_element_type=F32,
        )
        total = part if total is None else total + part
    for n in range(4):
        out_ref[n] = total[:, n * 128 : (n + 1) * 128].astype(out_ref.dtype)


def beside_kernel(x_ref, left_ref, blocks_ref, *outs):
    bands = [lax.rem(x_ref[0] + d, 4) for d in range(4)]
    total = None
    for h in range(4):
        blocks = [blocks_ref[block_of(x_ref[0], h, n), 0:352, :] for n in bands]
        part = lax.dot_general(
            left_ref[h * 352 : (h + 1) * 352, :],
            jnp.concatenate(blocks, axis=1),
            (((0,), (0,)), ((), ())),
            preferred_element_type=F32,
        )
        total = part if total is None else total + part
    for n, out in enumerate(outs):
        out[...] = total[:, n * 128 : (n + 1) * 128].astype(out.dtype)


def child_kernel(x_ref, left_ref, blocks_ref, out_ref):
    total = None
    for h in range(4):
        blocks = [blocks_ref[block_of(x_ref[0], h, n), 352:608, :] for n in range(4)]
        left = jnp.concatenate([left_ref[2 * h], left_ref[2 * h + 1]], axis=1)
        part = jnp.dot(left, jnp.concatenate(blocks, axis=1), preferred_element_type=F32)
        total = part if total is None else total + part
    for n in range(4):
        out_ref[n] = total[:, n * 128 : (n + 1) * 128].astype(out_ref.dtype)


def last_kernel(factor_ref, image_ref, out_ref):
    for x in range(4):
        total = None
        for y in range(4):
            n = (y * 4 + x) * 2
            left = jnp.concatenate([factor_ref[n], factor_ref[n + 1]], axis=1)
            part = lax.dot_general(
                left, image_ref[y], (((0,), (0,)), ((), ())), preferred_element_type=F32
            )
            total = part if total is None else total + part
        out_ref[x] = total.astype(out_ref.dtype)


def shift(value, by):
    return lax.ppermute(value, Z, [(i, (i + by) % 16) for i in range(16)])


def along(value, axis, by):
    return lax.ppermute(value, axis, [(i, (i + by) % 4) for i in range(4)])


def swap(value, first, second):
    pairs = [(a * 4 + b, b * 4 + a) for a in range(4) for b in range(4)]
    return lax.ppermute(value, (first, second), pairs)


def nearest(value):
    pairs = []
    for p in range(16):
        for n in range(4):
            plane = (p + (n - p + 1) % 4 - 1) % 16
            pairs.append((p * 4 + n, plane * 4 + p % 4))
    return lax.ppermute(value, ("zh", "zl", "x"), pairs)


def exchange(value, axis):
    return lax.all_to_all(value, axis, split_axis=0, concat_axis=0, tiled=True)


def after(value, *others):
    return lax.optimization_barrier((value, *others))[0]


def per_device(
    ancestor_cov,
    ancestor_pattern,
    parent_panel,
    parent_inverse,
    child_pattern,
    child_panel,
    child_inverse,
):
    z = lax.axis_index(Z)
    zl = lax.axis_index("zl")
    column = lax.axis_index(PLANE)
    place = lax.axis_index("x").astype(jnp.int32)[None]

    slab = lax.dynamic_slice_in_dim(parent_panel, column * 128, 128, 1)
    swapped = nearest(jnp.concatenate([slab, child_panel], axis=0))

    ancestor_keep = block_keep(ancestor_pattern, z * 352, 352, 5632)
    column_keep = block_keep(ancestor_pattern, column * 176, 176, 5632)
    child_keep = block_keep(child_pattern, z * 256, 256, 4096)
    child_column_keep = block_keep(child_pattern, column * 128, 128, 4096)
    cov = ancestor_cov * ancestor_keep[:, None].astype(BF) * column_keep[None, :].astype(BF)
    cov = cov.T

    classes = jnp.stack([(zl + 1) % 4, (zl + 3) % 4, (zl + 2) % 4, zl]).astype(jnp.int32)
    bundle = jax.ShapeDtypeStruct((4, 176, 256), BF)
    own, right, left, far = call(
        image_kernel,
        [jax.ShapeDtypeStruct((4, 176, 256), F32), bundle, bundle, bundle],
        [classes, cov, parent_panel],
        2 * 176 * 352 * 4096,
    )
    blocks = lax.all_gather(after(swapped, own), Z, axis=0)
    right, left = shift(right, 1), shift(left, -1)
    far = jnp.concatenate([shift(far[:2], 2), shift(far[2:], -2)], axis=0)
    image = own + right.astype(F32) + left.astype(F32) + far.astype(F32)

    zh = lax.axis_index("zh")
    near = [lax.dynamic_index_in_dim(image, (zh + d) % 4, 0, False) for d in range(4)]
    half = near[2].astype(BF)
    ahead, behind = along(half[:, :128], "zh", 1), along(half[:, 128:], "zh", 3)
    cov_wide = lax.all_gather(after(cov, half), ("y", "c"), axis=0, tiled=True)
    ahead = after(ahead, cov_wide)
    nothing = jnp.zeros((176, 128), F32)
    ahead = near[1] + jnp.concatenate([ahead.astype(F32), nothing], axis=1)
    behind = near[3] + jnp.concatenate([nothing, behind.astype(F32)], axis=1)
    ahead = along(ahead.astype(BF), "zh", 1)
    behind = along(behind.astype(BF), "zh", 3)
    image = (near[0] + ahead.astype(F32) + behind.astype(F32)).astype(BF)
    factor = swap(after(child_panel, image), "zh", "y")
    image_wide = lax.all_gather(image, ("y", "c"), axis=0, tiled=True)
    factor = lax.all_gather(after(factor, image_wide), PLANE, axis=0)

    (inner,) = call(
        panel_kernel,
        [jax.ShapeDtypeStruct((4, 256, 128), BF)],
        [place, image_wide, blocks],
        2 * 1408 * 256 * 512,
    )
    part = jax.ShapeDtypeStruct((352, 128), BF)
    besides = call(
        beside_kernel,
        [jax.ShapeDtypeStruct((352, 128), F32), part, part, part],
        [place, cov_wide, after(blocks, inner)],
        2 * 1408 * 352 * 512,
    )
    inner = jnp.sum(after(exchange(inner, "x"), besides[0]).astype(F32), axis=0)
    parent_diag = (parent_inverse.astype(F32) + inner).astype(BF)

    across = along(besides[2], "x", 2)
    diag_wide = parent_diag * child_column_keep[None, :].astype(BF)
    diag_wide = lax.all_gather(diag_wide, ("y", "c"), axis=0)
    (product,) = call(
        child_kernel,
        [jax.ShapeDtypeStruct((4, 256, 128), BF)],
        [place, after(diag_wide, across), blocks],
        2 * 1024 * 256 * 512,
    )
    moved = [along(after(besides[d], product), "x", d) for d in (1, 3)] + [across]
    product = jnp.sum(exchange(product, "x").astype(F32), axis=0)
    parent_child = (-product * child_keep[:, None].astype(F32)).astype(BF)

    child_wide = lax.all_gather(parent_child, "zh", axis=0)
    (inner,) = call(
        last_kernel,
        [jax.ShapeDtypeStruct((4, 256, 128), BF)],
        [factor, after(child_wide, *moved)],
        2 * 1024 * 1024 * 128,
    )
    inner = jnp.sum(exchange(inner, "zl").astype(F32), axis=0)
    product = besides[0] + sum(block.astype(F32) for block in moved)
    ancestor_block = (-product * ancestor_keep[:, None].astype(F32)).astype(BF)
    child_diag = (child_inverse.astype(F32) - inner).astype(BF)
    return (ancestor_block, parent_diag, parent_child, child_diag)


def solution(mesh):
    fine = Mesh(mesh.devices.reshape(4, 4, 4, 4, 2), ("zh", "zl", "y", "x", "c"))
    blocked = P(Z, PLANE)
    return jax.shard_map(
        per_device,
        mesh=fine,
        in_specs=(blocked, P(), P(Z, None), blocked, P(), blocked, blocked),
        out_specs=(blocked, blocked, blocked, blocked),
        check_vma=False,
    )
```

```python
import jax
import jax.numpy as jnp
from jax import lax
from jax.experimental import pallas as pl
from jax.experimental.pallas import tpu as pltpu
from jax.sharding import Mesh, PartitionSpec as P

BF = jnp.bfloat16
F32 = jnp.float32
VMEM = pl.BlockSpec(memory_space=pltpu.VMEM)
SMEM = pl.BlockSpec(memory_space=pltpu.SMEM)
Z = ("zh", "zl")
PLANE = ("y", "x", "c")


def block_keep(pattern, first_row, count, total_rows):
    block_rows = total_rows // pattern.shape[0]
    row_ids = first_row + lax.iota(jnp.int32, count)
    block_ids = lax.iota(jnp.int32, pattern.shape[0])
    matches = row_ids[:, None] // block_rows == block_ids[None, :]
    return jnp.sum(jnp.where(matches, pattern[None, :], 0), axis=1)


def call(kernel, outs, args, flops):
    specs = [SMEM if a.dtype == jnp.int32 else VMEM for a in args]
    size = sum(a.size * a.dtype.itemsize for a in args)
    size += sum(o.size * o.dtype.itemsize for o in outs)
    return pl.pallas_call(
        kernel,
        out_shape=outs,
        in_specs=specs,
        out_specs=[VMEM] * len(outs),
        compiler_params=pltpu.CompilerParams(vmem_limit_bytes=20 * 1024 * 1024),
        cost_estimate=pl.CostEstimate(flops=flops, bytes_accessed=size, transcendentals=0),
    )(*args)


def image_kernel(classes, at_ref, panel_ref, own_ref, right_ref, left_ref, far_ref):
    at = at_ref[...]
    for n, out in enumerate((right_ref, left_ref, far_ref, own_ref)):
        for rh in range(4):
            start = pl.multiple_of((4 * rh + classes[n]) * 256, 256)
            block = jnp.dot(at, panel_ref[:, pl.ds(start, 256)], preferred_element_type=F32)
            out[rh] = block.astype(out.dtype)


def block_of(x, h, n):
    over = lax.rem(x - n + 6, 4) - 2 + n - x
    return lax.rem(4 * h - over + 16, 16) + n


def panel_kernel(x_ref, left_ref, blocks_ref, out_ref):
    rows = left_ref.shape[0] // 4
    total = None
    for h in range(4):
        blocks = [blocks_ref[block_of(x_ref[0], h, n), 0:352, :] for n in range(4)]
        part = lax.dot_general(
            left_ref[h * rows : (h + 1) * rows, :],
            jnp.concatenate(blocks, axis=1),
            (((0,), (0,)), ((), ())),
            preferred_element_type=F32,
        )
        total = part if total is None else total + part
    for n in range(4):
        out_ref[n] = total[:, n * 128 : (n + 1) * 128].astype(out_ref.dtype)


def beside_kernel(x_ref, left_ref, blocks_ref, *outs):
    bands = [lax.rem(x_ref[0] + d, 4) for d in range(4)]
    total = None
    for h in range(4):
        blocks = [blocks_ref[block_of(x_ref[0], h, n), 0:352, :] for n in bands]
        part = lax.dot_general(
            left_ref[h * 352 : (h + 1) * 352, :],
            jnp.concatenate(blocks, axis=1),
            (((0,), (0,)), ((), ())),
            preferred_element_type=F32,
        )
        total = part if total is None else total + part
    for n, out in enumerate(outs):
        out[...] = total[:, n * 128 : (n + 1) * 128].astype(out.dtype)


def child_kernel(x_ref, left_ref, blocks_ref, out_ref):
    total = None
    for h in range(4):
        blocks = [blocks_ref[block_of(x_ref[0], h, n), 352:608, :] for n in range(4)]
        left = jnp.concatenate([left_ref[2 * h], left_ref[2 * h + 1]], axis=1)
        part = jnp.dot(left, jnp.concatenate(blocks, axis=1), preferred_element_type=F32)
        total = part if total is None else total + part
    for n in range(4):
        out_ref[n] = total[:, n * 128 : (n + 1) * 128].astype(out_ref.dtype)


def last_kernel(factor_ref, image_ref, out_ref):
    for x in range(4):
        total = None
        for y in range(4):
            n = (y * 4 + x) * 2
            left = jnp.concatenate([factor_ref[n], factor_ref[n + 1]], axis=1)
            part = lax.dot_general(
                left, image_ref[y], (((0,), (0,)), ((), ())), preferred_element_type=F32
            )
            total = part if total is None else total + part
        out_ref[x] = total.astype(out_ref.dtype)


def shift(value, by):
    return lax.ppermute(value, Z, [(i, (i + by) % 16) for i in range(16)])


def along(value, axis, by):
    return lax.ppermute(value, axis, [(i, (i + by) % 4) for i in range(4)])


def swap(value, first, second):
    pairs = [(a * 4 + b, b * 4 + a) for a in range(4) for b in range(4)]
    return lax.ppermute(value, (first, second), pairs)


def nearest(value):
    pairs = []
    for p in range(16):
        for n in range(4):
            plane = (p + (n - p + 1) % 4 - 1) % 16
            pairs.append((p * 4 + n, plane * 4 + p % 4))
    return lax.ppermute(value, ("zh", "zl", "x"), pairs)


def exchange(value, axis):
    return lax.all_to_all(value, axis, split_axis=0, concat_axis=0, tiled=True)


def after(value, *others):
    return lax.optimization_barrier((value, *others))[0]


def per_device(
    ancestor_cov,
    ancestor_pattern,
    parent_panel,
    parent_inverse,
    child_pattern,
    child_panel,
    child_inverse,
):
    z = lax.axis_index(Z)
    zl = lax.axis_index("zl")
    column = lax.axis_index(PLANE)
    place = lax.axis_index("x").astype(jnp.int32)[None]

    slab = lax.dynamic_slice_in_dim(parent_panel, column * 128, 128, 1)
    swapped = nearest(jnp.concatenate([slab, child_panel], axis=0))

    ancestor_keep = block_keep(ancestor_pattern, z * 352, 352, 5632)
    column_keep = block_keep(ancestor_pattern, column * 176, 176, 5632)
    child_keep = block_keep(child_pattern, z * 256, 256, 4096)
    child_column_keep = block_keep(child_pattern, column * 128, 128, 4096)
    cov = ancestor_cov * ancestor_keep[:, None].astype(BF) * column_keep[None, :].astype(BF)
    cov = cov.T

    classes = jnp.stack([(zl + 1) % 4, (zl + 3) % 4, (zl + 2) % 4, zl]).astype(jnp.int32)
    bundle = jax.ShapeDtypeStruct((4, 176, 256), BF)
    own, right, left, far = call(
        image_kernel,
        [jax.ShapeDtypeStruct((4, 176, 256), F32), bundle, bundle, bundle],
        [classes, cov, parent_panel],
        2 * 176 * 352 * 4096,
    )
    blocks = lax.all_gather(after(swapped, own), Z, axis=0)
    right, left = shift(right, 1), shift(left, -1)
    far = jnp.concatenate([shift(far[:2], 2), shift(far[2:], -2)], axis=0)
    cov_wide = lax.all_gather(after(cov, own), ("y", "c"), axis=0, tiled=True)
    right = after(right, cov_wide)
    image = own + right.astype(F32) + left.astype(F32) + far.astype(F32)

    zh = lax.axis_index("zh")
    near = [lax.dynamic_index_in_dim(image, (zh + d) % 4, 0, False) for d in range(4)]
    half = near[2].astype(BF)
    ahead, behind = along(half[:, :128], "zh", 1), along(half[:, 128:], "zh", 3)
    nothing = jnp.zeros((176, 128), F32)
    ahead = near[1] + jnp.concatenate([ahead.astype(F32), nothing], axis=1)
    behind = near[3] + jnp.concatenate([nothing, behind.astype(F32)], axis=1)
    ahead = along(ahead.astype(BF), "zh", 1)
    behind = along(behind.astype(BF), "zh", 3)
    image = (near[0] + ahead.astype(F32) + behind.astype(F32)).astype(BF)
    factor = swap(after(child_panel, image), "zh", "y")
    image_wide = lax.all_gather(image, ("y", "c"), axis=0, tiled=True)
    factor = lax.all_gather(after(factor, image_wide), PLANE, axis=0)

    (inner,) = call(
        panel_kernel,
        [jax.ShapeDtypeStruct((4, 256, 128), BF)],
        [place, image_wide, blocks],
        2 * 1408 * 256 * 512,
    )
    part = jax.ShapeDtypeStruct((352, 128), BF)
    besides = call(
        beside_kernel,
        [jax.ShapeDtypeStruct((352, 128), F32), part, part, part],
        [place, cov_wide, after(blocks, inner)],
        2 * 1408 * 352 * 512,
    )
    inner = jnp.sum(after(exchange(inner, "x"), besides[0]).astype(F32), axis=0)
    parent_diag = (parent_inverse.astype(F32) + inner).astype(BF)

    across = along(besides[2], "x", 2)
    diag_wide = parent_diag * child_column_keep[None, :].astype(BF)
    diag_wide = lax.all_gather(diag_wide, ("y", "c"), axis=0)
    (product,) = call(
        child_kernel,
        [jax.ShapeDtypeStruct((4, 256, 128), BF)],
        [place, after(diag_wide, across), blocks],
        2 * 1024 * 256 * 512,
    )
    moved = [along(after(besides[d], product), "x", d) for d in (1, 3)] + [across]
    product = jnp.sum(exchange(product, "x").astype(F32), axis=0)
    parent_child = (-product * child_keep[:, None].astype(F32)).astype(BF)

    child_wide = lax.all_gather(parent_child, "zh", axis=0)
    (inner,) = call(
        last_kernel,
        [jax.ShapeDtypeStruct((4, 256, 128), BF)],
        [factor, after(child_wide, *moved)],
        2 * 1024 * 1024 * 128,
    )
    inner = jnp.sum(exchange(inner, "zl").astype(F32), axis=0)
    product = besides[0] + sum(block.astype(F32) for block in moved)
    ancestor_block = (-product * ancestor_keep[:, None].astype(F32)).astype(BF)
    child_diag = (child_inverse.astype(F32) - inner).astype(BF)
    return (ancestor_block, parent_diag, parent_child, child_diag)


def solution(mesh):
    fine = Mesh(mesh.devices.reshape(4, 4, 4, 4, 2), ("zh", "zl", "y", "x", "c"))
    blocked = P(Z, PLANE)
    return jax.shard_map(
        per_device,
        mesh=fine,
        in_specs=(blocked, P(), P(Z, None), blocked, P(), blocked, blocked),
        out_specs=(blocked, blocked, blocked, blocked),
        check_vma=False,
    )
```

```python
import jax
import jax.numpy as jnp
from jax import lax
from jax.experimental import pallas as pl
from jax.experimental.pallas import tpu as pltpu
from jax.sharding import Mesh, PartitionSpec as P

BF = jnp.bfloat16
F32 = jnp.float32
VMEM = pl.BlockSpec(memory_space=pltpu.VMEM)
SMEM = pl.BlockSpec(memory_space=pltpu.SMEM)
Z = ("zh", "zl")
PLANE = ("y", "x", "c")


def block_keep(pattern, first_row, count, total_rows):
    block_rows = total_rows // pattern.shape[0]
    row_ids = first_row + lax.iota(jnp.int32, count)
    block_ids = lax.iota(jnp.int32, pattern.shape[0])
    matches = row_ids[:, None] // block_rows == block_ids[None, :]
    return jnp.sum(jnp.where(matches, pattern[None, :], 0), axis=1)


def call(kernel, outs, args, flops):
    specs = [SMEM if a.dtype == jnp.int32 else VMEM for a in args]
    size = sum(a.size * a.dtype.itemsize for a in args)
    size += sum(o.size * o.dtype.itemsize for o in outs)
    return pl.pallas_call(
        kernel,
        out_shape=outs,
        in_specs=specs,
        out_specs=[VMEM] * len(outs),
        compiler_params=pltpu.CompilerParams(vmem_limit_bytes=20 * 1024 * 1024),
        cost_estimate=pl.CostEstimate(flops=flops, bytes_accessed=size, transcendentals=0),
    )(*args)


def image_kernel(classes, at_ref, panel_ref, own_ref, right_ref, left_ref, far_ref):
    at = at_ref[...]
    for n, out in enumerate((right_ref, left_ref, far_ref, own_ref)):
        for rh in range(4):
            start = pl.multiple_of((4 * rh + classes[n]) * 256, 256)
            block = jnp.dot(at, panel_ref[:, pl.ds(start, 256)], preferred_element_type=F32)
            out[rh] = block.astype(out.dtype)


def block_of(x, h, n):
    over = lax.rem(x - n + 6, 4) - 2 + n - x
    return lax.rem(4 * h - over + 16, 16) + n


def panel_kernel(x_ref, left_ref, blocks_ref, out_ref):
    rows = left_ref.shape[0] // 4
    total = None
    for h in range(4):
        blocks = [blocks_ref[block_of(x_ref[0], h, n), 0:352, :] for n in range(4)]
        part = lax.dot_general(
            left_ref[h * rows : (h + 1) * rows, :],
            jnp.concatenate(blocks, axis=1),
            (((0,), (0,)), ((), ())),
            preferred_element_type=F32,
        )
        total = part if total is None else total + part
    for n in range(4):
        out_ref[n] = total[:, n * 128 : (n + 1) * 128].astype(out_ref.dtype)


def beside_kernel(x_ref, left_ref, blocks_ref, *outs):
    bands = [lax.rem(x_ref[0] + d, 4) for d in range(4)]
    total = None
    for h in range(4):
        blocks = [blocks_ref[block_of(x_ref[0], h, n), 0:352, :] for n in bands]
        part = lax.dot_general(
            left_ref[h * 352 : (h + 1) * 352, :],
            jnp.concatenate(blocks, axis=1),
            (((0,), (0,)), ((), ())),
            preferred_element_type=F32,
        )
        total = part if total is None else total + part
    for n, out in enumerate(outs):
        out[...] = total[:, n * 128 : (n + 1) * 128].astype(out.dtype)


def child_kernel(x_ref, left_ref, blocks_ref, out_ref):
    total = None
    for h in range(4):
        blocks = [blocks_ref[block_of(x_ref[0], h, n), 352:608, :] for n in range(4)]
        left = jnp.concatenate([left_ref[2 * h], left_ref[2 * h + 1]], axis=1)
        part = jnp.dot(left, jnp.concatenate(blocks, axis=1), preferred_element_type=F32)
        total = part if total is None else total + part
    for n in range(4):
        out_ref[n] = total[:, n * 128 : (n + 1) * 128].astype(out_ref.dtype)


def last_kernel(factor_ref, image_ref, out_ref):
    total = None
    for y in range(4):
        left = jnp.concatenate([factor_ref[y, 0], factor_ref[y, 1]], axis=1)
        part = lax.dot_general(
            left, image_ref[y], (((0,), (0,)), ((), ())), preferred_element_type=F32
        )
        total = part if total is None else total + part
    out_ref[0] = total.astype(out_ref.dtype)


def last_product(factor, image):
    return pl.pallas_call(
        last_kernel,
        grid=(4,),
        out_shape=jax.ShapeDtypeStruct((4, 256, 128), BF),
        in_specs=[
            pl.BlockSpec((4, 2, 256, 128), lambda x: (0, x, 0, 0)),
            pl.BlockSpec((4, 256, 128), lambda x: (0, 0, 0)),
        ],
        out_specs=pl.BlockSpec((1, 256, 128), lambda x: (x, 0, 0)),
        compiler_params=pltpu.CompilerParams(vmem_limit_bytes=60 * 1024 * 1024),
        cost_estimate=pl.CostEstimate(
            flops=2 * 1024 * 1024 * 128, bytes_accessed=2621440, transcendentals=0
        ),
    )(factor.reshape(4, 8, 256, 128), image)


def shift(value, by):
    return lax.ppermute(value, Z, [(i, (i + by) % 16) for i in range(16)])


def along_x(value, by):
    return lax.ppermute(value, "x", [(i, (i + by) % 4) for i in range(4)])


def swap(value, first, second):
    pairs = [(a * 4 + b, b * 4 + a) for a in range(4) for b in range(4)]
    return lax.ppermute(value, (first, second), pairs)


def nearest(value):
    pairs = []
    for p in range(16):
        for n in range(4):
            plane = (p + (n - p + 1) % 4 - 1) % 16
            pairs.append((p * 4 + n, plane * 4 + p % 4))
    return lax.ppermute(value, ("zh", "zl", "x"), pairs)


def exchange(value, axis):
    return lax.all_to_all(value, axis, split_axis=0, concat_axis=0, tiled=True)


def after(value, *others):
    return lax.optimization_barrier((value, *others))[0]


def per_device(
    ancestor_cov,
    ancestor_pattern,
    parent_panel,
    parent_inverse,
    child_pattern,
    child_panel,
    child_inverse,
):
    z = lax.axis_index(Z)
    zl = lax.axis_index("zl")
    column = lax.axis_index(PLANE)
    place = lax.axis_index("x").astype(jnp.int32)[None]

    slab = lax.dynamic_slice_in_dim(parent_panel, column * 128, 128, 1)
    swapped = nearest(jnp.concatenate([slab, child_panel], axis=0))

    ancestor_keep = block_keep(ancestor_pattern, z * 352, 352, 5632)
    column_keep = block_keep(ancestor_pattern, column * 176, 176, 5632)
    child_keep = block_keep(child_pattern, z * 256, 256, 4096)
    child_column_keep = block_keep(child_pattern, column * 128, 128, 4096)
    cov = ancestor_cov * ancestor_keep[:, None].astype(BF) * column_keep[None, :].astype(BF)
    cov = cov.T

    classes = jnp.stack([(zl + 1) % 4, (zl + 3) % 4, (zl + 2) % 4, zl]).astype(jnp.int32)
    bundle = jax.ShapeDtypeStruct((4, 176, 256), BF)
    own, right, left, far = call(
        image_kernel,
        [jax.ShapeDtypeStruct((4, 176, 256), F32), bundle, bundle, bundle],
        [classes, cov, parent_panel],
        2 * 176 * 352 * 4096,
    )
    blocks = lax.all_gather(after(swapped, own), Z, axis=0)
    right, left = shift(right, 1), shift(left, -1)
    far = jnp.concatenate([shift(far[:2], 2), shift(far[2:], -2)], axis=0)
    image = own + right.astype(F32) + left.astype(F32) + far.astype(F32)
    image = image.astype(BF)

    cov_wide = lax.all_gather(after(cov, image), ("y", "c"), axis=0, tiled=True)
    image = after(exchange(image, "zh"), cov_wide)
    image = jnp.sum(image.astype(F32), axis=0).astype(BF)
    factor = swap(after(child_panel, image), "zh", "y")
    image_wide = lax.all_gather(image, ("y", "c"), axis=0, tiled=True)
    factor = lax.all_gather(after(factor, image_wide), PLANE, axis=0)

    (inner,) = call(
        panel_kernel,
        [jax.ShapeDtypeStruct((4, 256, 128), BF)],
        [place, image_wide, blocks],
        2 * 1408 * 256 * 512,
    )
    part = jax.ShapeDtypeStruct((352, 128), BF)
    besides = call(
        beside_kernel,
        [jax.ShapeDtypeStruct((352, 128), F32), part, part, part],
        [place, cov_wide, after(blocks, inner)],
        2 * 1408 * 352 * 512,
    )
    inner = jnp.sum(after(exchange(inner, "x"), besides[0]).astype(F32), axis=0)
    parent_diag = (parent_inverse.astype(F32) + inner).astype(BF)

    across = along_x(besides[2], 2)
    diag_wide = parent_diag * child_column_keep[None, :].astype(BF)
    diag_wide = lax.all_gather(diag_wide, ("y", "c"), axis=0)
    (product,) = call(
        child_kernel,
        [jax.ShapeDtypeStruct((4, 256, 128), BF)],
        [place, after(diag_wide, across), blocks],
        2 * 1024 * 256 * 512,
    )
    moved = [along_x(after(besides[d], product), d) for d in (1, 3)] + [across]
    product = jnp.sum(exchange(product, "x").astype(F32), axis=0)
    parent_child = (-product * child_keep[:, None].astype(F32)).astype(BF)

    child_wide = lax.all_gather(parent_child, "zh", axis=0)
    inner = last_product(factor, after(child_wide, *moved))
    inner = jnp.sum(exchange(inner, "zl").astype(F32), axis=0)
    product = besides[0] + sum(block.astype(F32) for block in moved)
    ancestor_block = (-product * ancestor_keep[:, None].astype(F32)).astype(BF)
    child_diag = (child_inverse.astype(F32) - inner).astype(BF)
    return (ancestor_block, parent_diag, parent_child, child_diag)


def solution(mesh):
    fine = Mesh(mesh.devices.reshape(4, 4, 4, 4, 2), ("zh", "zl", "y", "x", "c"))
    blocked = P(Z, PLANE)
    return jax.shard_map(
        per_device,
        mesh=fine,
        in_specs=(blocked, P(), P(Z, None), blocked, P(), blocked, blocked),
        out_specs=(blocked, blocked, blocked, blocked),
        check_vma=False,
    )
```
